256 devices in a mesh: grp: 4 (over x), pair: 64 (over z, y, core).
Axes of the slice: x: 4, y: 4, z: 8, core: 2. Of those that a mesh axis runs over, the one named last changes fastest.
Arguments:
- blocks: float32 [1024, 128, 128], P(('grp', 'pair')), may hold values from -24 to 24
- block_home: int32 [1024], P(('grp', 'pair')), may hold values from 0 to 1
- block_group: int32 [1024, 1], P(('grp', 'pair')), may hold values from 0 to 3; in each aligned block of 4 rows (0 to 3, 4 to 7, ...) at most 2 rows name the same one
- block_slot: int32 [1024], P(('grp', 'pair')), may hold values from 0 to 1
- pair_funcs: int32 [2, 65536], P(None, ('grp', 'pair')), may hold values from 0 to 1535
- occ_coef: float32 [1536, 16], replicated, may hold values from -0.4 to 0.4
- vir_coef: float32 [1536, 128], replicated, may hold values from -0.4 to 0.4
Outputs:
- half_ints: float32 [65536, 2048], P(('grp', 'pair'))
- orbital_ints: float32 [2048, 2048], P(('grp', 'pair'))
The draws below stay inside these ranges and needn't reach their ends.
Inputs may be any that keep to these rules, and one draw needn't show every extreme that they name: `block_group`: in the 4 blocks of one device no group is named by more than 2 blocks.
All inputs are finite; a program needn't handle non-finite values.
Results may differ from the reference program's by a relative error of at most 0.0001.
Values sent between devices are 32-bit elements; how exact they have to be, the bound alone decides.
A program may use at most 192 MiB of HBM per device.

```python
import math
import jax
import jax.numpy as jnp
import numpy as np
from jax import lax

NB = 1536
NOCC = 16
NVIR = 128
TILE = 128
TILES_DEV = 2
BLOCKS_DEV = 4
CAP = 2
TILES = 512
BLOCKS = 1024
N_GRP = 4
N_PAIR = 64


def with_ends(array, key, least, largest):
    dims = array.shape
    spot = [jax.random.randint(jax.random.fold_in(key, axis), (), 0, dims[axis]) for axis in range(len(dims))]
    array = array.at[tuple(spot)].set(least)
    longest = dims.index(max(dims))
    spot[longest] = (spot[longest] + 1) % dims[longest]
    return array.at[tuple(spot)].set(largest)


def level_of(own_key, shape, cuts, least, high):
    factor_of = 1.0
    for position, parts in cuts:
        draws = jax.random.uniform(jax.random.fold_in(jax.random.fold_in(own_key, 6), position), (parts,), jnp.float32, least / len(cuts), high / len(cuts))
        factor_of = factor_of * jnp.repeat(jnp.exp(draws), shape[position] // parts).reshape((-1,) + (1,) * (len(shape) - 1 - position))
    return factor_of


def assign_block(rng, own, number, rows, amount, top, reach, lean):
    ranking = jax.random.permutation(rng, amount)
    packed, common = portions_of(amount, rows * top, reach, lean, True), portions_of(amount, rows * top, reach, lean, False)
    places = jnp.arange(amount)

    def named(tallies, rotation):
        used = int((tallies > 0).sum())
        fixed = max(1, used // 4)
        passed = fixed + (places - fixed + rotation * (used - fixed)) % max(1, amount - fixed)
        return jnp.zeros((amount,), jnp.int32).at[ranking[jnp.where(places < fixed, places, passed)]].set(jnp.asarray(tallies, jnp.int32))

    tallies = jnp.where(number % 4 == 0, named(packed, number // 4), named(common, number - number // 4 - 1))
    mixed = jax.random.permutation(jax.random.fold_in(own, 3), amount)
    giver, receiver = mixed[0:amount // 2 * 2:2], mixed[1:amount // 2 * 2:2]
    margin = jnp.minimum(tallies[giver] - 1, reach - tallies[receiver]) // 2
    margin = jnp.where((giver == ranking[0]) | (receiver == ranking[0]) | (tallies[receiver] == 0), 0, jnp.maximum(margin, 0))
    passed = jax.random.randint(jax.random.fold_in(own, 4), (amount // 2,), 0, 1 << 20) % (margin + 1)
    tallies = tallies.at[giver].add(-passed).at[receiver].add(passed)
    items = jnp.searchsorted(jnp.cumsum(tallies), jnp.arange(rows * top), side="right").astype(jnp.int32)
    listing = items.reshape(top, rows).T
    listing = listing[jax.random.permutation(jax.random.fold_in(own, 1), rows)]
    rotation = jax.random.randint(jax.random.fold_in(own, 2), (rows, 1), 0, top)
    return jnp.take_along_axis(listing, (jnp.arange(top)[None, :] + rotation) % top, axis=1)


def portions_of(amount, total, bound, slope, full):
    portions = [(1 << 20) // math.isqrt(rank ** slope) + 1 for rank in range(1, amount + 1)]
    largest = bound if full else min(bound, max(-(-total // amount), total * portions[0] // sum(portions)))
    least = 1 if total - largest >= amount - 1 else 0
    counts, spare = [largest] + [least] * (amount - 1), total - largest - least * (amount - 1)
    while spare > 0:
        movable = [i for i in range(1, amount) if counts[i] < largest] or [i for i in range(1, amount) if counts[i] < bound]
        whole, remaining = sum([portions[i] for i in movable]), spare
        for i in movable:
            addition = min(bound - counts[i], max(1, remaining * portions[i] // whole), spare)
            counts[i] = counts[i] + addition
            spare = spare - addition
    return np.array(counts)


def bell_draw(own_key, extent, scale, limit, cuts=(), held_as=jnp.bfloat16):
    loudness = level_of(own_key, extent, cuts, -0.22, 0.18) if cuts else 1.0
    entries = jax.random.normal(own_key, extent, jnp.float32) * scale * loudness
    return jnp.minimum(jnp.maximum(entries, -limit), limit).astype(held_as)


def setup_inputs(seed: int = 0) -> dict:
    splits = jax.random.split(jax.random.key(seed), 8)
    blocks = bell_draw(splits[0], (BLOCKS, TILE, TILE), 4.0, 24.0, ((0, 256),), jnp.float32)
    block_home = with_ends(jax.random.randint(splits[1], (BLOCKS,), 0, TILES_DEV), jax.random.fold_in(splits[1], 1), 0, TILES_DEV - 1).astype(jnp.int32)
    block_group_keys = jax.random.split(jax.random.fold_in(splits[2], 1), BLOCKS // BLOCKS_DEV)
    block_group_turns = jax.random.permutation(jax.random.fold_in(splits[2], 3), BLOCKS // BLOCKS_DEV)
    block_group = jax.vmap(lambda own, number: assign_block(jax.random.fold_in(splits[2], 2), own, number, BLOCKS_DEV, N_GRP, 1, CAP, 2))(block_group_keys, block_group_turns).reshape((BLOCKS, 1))
    block_slot = with_ends(jax.random.randint(splits[3], (BLOCKS,), 0, TILES_DEV), jax.random.fold_in(splits[3], 1), 0, TILES_DEV - 1).astype(jnp.int32)
    pair_funcs = with_ends(jax.random.randint(splits[4], (2, TILES * TILE), 0, NB), jax.random.fold_in(splits[4], 1), 0, NB - 1).astype(jnp.int32)
    occ_coef = bell_draw(splits[5], (NB, NOCC), 0.0625, 0.4, (), jnp.float32)
    vir_coef = bell_draw(splits[6], (NB, NVIR), 0.0625, 0.4, (), jnp.float32)
    return {"blocks": blocks, "block_home": block_home, "block_group": block_group, "block_slot": block_slot, "pair_funcs": pair_funcs, "occ_coef": occ_coef, "vir_coef": vir_coef}


def orbital_table(rows_p, rows_q, occ_coef, vir_coef):
    occ_p = jnp.take(occ_coef, rows_p, axis=0)
    occ_q = jnp.take(occ_coef, rows_q, axis=0)
    vir_p = jnp.take(vir_coef, rows_p, axis=0)
    vir_q = jnp.take(vir_coef, rows_q, axis=0)
    table = occ_p[:, :, None] * vir_q[:, None, :] + occ_q[:, :, None] * vir_p[:, None, :]
    return table.reshape(rows_p.shape[0], -1)


def reference(blocks, block_home, block_group, block_slot, pair_funcs, occ_coef, vir_coef):
    highest = lax.Precision.HIGHEST
    table = orbital_table(pair_funcs[0], pair_funcs[1], occ_coef, vir_coef)
    width = table.shape[1]
    tables = table.reshape(-1, TILE, width)
    count = blocks.shape[0]
    index = jnp.arange(count, dtype=jnp.int32)
    device = index // BLOCKS_DEV
    home_tile = (device * TILES_DEV + block_home).astype(jnp.int32)
    partner_tile = ((block_group[:, 0] * N_PAIR + device % N_PAIR) * TILES_DEV + block_slot).astype(jnp.int32)

    def add_block(step, half):
        block = blocks[step]
        home = home_tile[step]
        partner = partner_tile[step]
        forward = jnp.dot(block, tables[partner], precision=highest, preferred_element_type=jnp.float32)
        mirror = jnp.dot(block.T, tables[home], precision=highest, preferred_element_type=jnp.float32)
        half = half.at[home].add(forward)
        return half.at[partner].add(mirror)

    half = lax.fori_loop(0, count, add_block, jnp.zeros(tables.shape, jnp.float32))
    flat = half.reshape(-1, width)
    orbital = lax.dot_general(flat, table, (((0,), (0,)), ((), ())), precision=highest, preferred_element_type=jnp.float32)
    return flat, orbital
```

```python
import functools

import jax
import jax.numpy as jnp
from jax import lax
from jax.experimental import pallas as pl
from jax.experimental.pallas import tpu as pltpu
from jax.sharding import PartitionSpec as P

F32, BF16 = jnp.float32, jnp.bfloat16


def split(value):
    high = value.astype(BF16)
    return high, (value - high.astype(F32)).astype(BF16)


def dot(lhs, rhs, contract):
    return lax.dot_general(lhs, rhs, (contract, ((), ())), preferred_element_type=F32)


NN, NT = ((1,), (0,)), ((1,), (1,))


def dot3(lh, ll, rh, rl, contract):
    return dot(lh, rh, contract) + (dot(lh, rl, contract) + dot(ll, rh, contract))


def pack_coef(occ_ref, vir_ref, coef_ref):
    n_occ, n_vir = occ_ref.shape[1], vir_ref.shape[1]
    width = n_vir + n_occ
    coef_ref[:n_vir], coef_ref[width : width + n_vir] = split(vir_ref[...].T)
    coef_ref[n_vir:width], coef_ref[width + n_vir :] = split(occ_ref[...].T)


def gather_table(coef_ref, funcs_ref, tab_h, tab_l, n_occ, n_vir, step):
    nb = coef_ref.shape[1]
    width = n_vir + n_occ
    rows = funcs_ref.shape[1]

    def body(c, carry):
        cols = pl.ds(pl.multiple_of(c * step, step), step)
        got = []
        for f in range(2):
            func = funcs_ref[f : f + 1, cols]
            hot = lax.broadcasted_iota(jnp.int32, (nb, step), 0) == func
            hot = jnp.where(hot, 1.0, 0.0).astype(BF16)
            both = dot(coef_ref[...], hot, NN)
            got.append(both[:width] + both[width:])
        (vir_p, occ_p), (vir_q, occ_q) = [(g[:n_vir], g[n_vir:]) for g in got]
        for i in range(n_occ):
            entry = occ_p[i : i + 1] * vir_q + occ_q[i : i + 1] * vir_p
            high, low = split(entry)
            tab_h[i * n_vir : (i + 1) * n_vir, cols] = high
            tab_l[i * n_vir : (i + 1) * n_vir, cols] = low
        return carry

    lax.fori_loop(0, rows // step, body, 0)


def build_matrix(home_ref, part_ref, blocks_ref, flip, mat_h, mat_l, tiles_dev):
    count, tile, _ = blocks_ref.shape
    n_tiles = mat_h.shape[0] // tile
    per_dev = count * tiles_dev // n_tiles
    for b in range(count):
        flip[b] = blocks_ref[b].T

    def body(step, carry):
        h, t = step // n_tiles, lax.rem(step, n_tiles)
        dev_h, dev_t = h // tiles_dev, t // tiles_dev
        total = jnp.zeros((tile, tile), F32)
        for j in range(per_dev):
            b = dev_h * per_dev + j
            here = jnp.logical_and(home_ref[b] == h, part_ref[b] == t)
            total = total + jnp.where(here, blocks_ref[b], 0.0)
            b = dev_t * per_dev + j
            here = jnp.logical_and(home_ref[b] == t, part_ref[b] == h)
            total = total + jnp.where(here, flip[b], 0.0)
        high, low = split(total)
        rows = pl.ds(pl.multiple_of(h * tile, tile), tile)
        cols = pl.ds(pl.multiple_of(t * tile, tile), tile)
        mat_h[rows, cols] = high
        mat_l[rows, cols] = low
        return carry

    lax.fori_loop(0, n_tiles * n_tiles, body, 0)


def column_kernel(n_occ, n_vir, tiles_dev, home_ref, part_ref, funcs_ref, occ_ref, vir_ref, blocks_ref, half_ref, part_out,
                  coef_ref, tab_h, tab_l, mat_h, mat_l, flip, g_h, g_l):
    grp = lax.axis_index("grp")
    width, rows = tab_h.shape
    mine = part_out.shape[0]
    own = half_ref.shape[0]
    pack_coef(occ_ref, vir_ref, coef_ref)
    gather_table(coef_ref, funcs_ref, tab_h, tab_l, n_occ, n_vir, 256)
    build_matrix(home_ref, part_ref, blocks_ref, flip, mat_h, mat_l, tiles_dev)
    share = pl.ds(pl.multiple_of(grp * mine, mine), mine)

    def make_g(c, carry):
        cols = pl.ds(pl.multiple_of(c * 256, 256), 256)
        g = dot3(tab_h[share, :], tab_l[share, :], mat_h[:, cols], mat_l[:, cols], NN)
        g_h[:, cols], g_l[:, cols] = split(g)
        return carry

    lax.fori_loop(0, rows // 256, make_g, 0)
    local = pl.ds(pl.multiple_of(grp * own, own), own)

    def outputs(c, carry):
        cols = pl.ds(pl.multiple_of(c * 256, 256), 256)
        part_out[:, cols] = dot3(g_h[...], g_l[...], tab_h[cols, :], tab_l[cols, :], NT)
        half_ref[:, cols] = dot3(mat_h[local, :], mat_l[local, :], tab_h[cols, :], tab_l[cols, :], NT)
        return carry

    lax.fori_loop(0, width // 256, outputs, 0)


def on_device(blocks, block_home, block_group, block_slot, pair_funcs, occ_coef, vir_coef):
    n_grp = lax.axis_size("grp")
    grp = lax.axis_index("grp")
    tile = blocks.shape[1]
    own = pair_funcs.shape[1]
    tiles_dev = own // tile
    n_occ, n_vir = occ_coef.shape[1], vir_coef.shape[1]
    width = n_occ * n_vir
    rows = own * n_grp
    count = blocks.shape[0] * n_grp
    mine = width // n_grp
    home = grp * tiles_dev + block_home
    part = block_group[:, 0] * tiles_dev + block_slot
    funcs = lax.all_gather(pair_funcs, "grp", axis=1, tiled=True)
    codes = lax.all_gather(jnp.stack([home, part]), "grp", axis=1, tiled=True)
    every = lax.all_gather(blocks, "grp", axis=0, tiled=True)
    vmem = pl.BlockSpec(memory_space=pltpu.VMEM)
    smem = pl.BlockSpec(memory_space=pltpu.SMEM)
    half, partial = pl.pallas_call(
        functools.partial(column_kernel, n_occ, n_vir, tiles_dev),
        out_shape=(jax.ShapeDtypeStruct((own, width), F32), jax.ShapeDtypeStruct((mine, width), F32)),
        in_specs=[smem, smem, vmem, vmem, vmem, vmem],
        out_specs=(vmem, vmem),
        scratch_shapes=[
            pltpu.VMEM((2 * (n_occ + n_vir), occ_coef.shape[0]), BF16),
            pltpu.VMEM((width, rows), BF16),
            pltpu.VMEM((width, rows), BF16),
            pltpu.VMEM((rows, rows), BF16),
            pltpu.VMEM((rows, rows), BF16),
            pltpu.VMEM((count, tile, tile), F32),
            pltpu.VMEM((mine, rows), BF16),
            pltpu.VMEM((mine, rows), BF16),
        ],
        compiler_params=pltpu.CompilerParams(vmem_limit_bytes=56 * 2**20),
    )(codes[0], codes[1], funcs, occ_coef, vir_coef, every)
    return half, lax.psum_scatter(partial, "pair", scatter_dimension=0, tiled=True)


def solution(mesh):
    both = ("grp", "pair")
    placed = (P(both, None, None), P(both), P(both, None), P(both), P(None, both), P(), P())
    return jax.shard_map(
        on_device,
        mesh=mesh,
        in_specs=placed,
        out_specs=(P(both, None), P(both, None)),
        check_vma=False,
    )
```

```python
import functools

import jax
import jax.numpy as jnp
from jax import lax
from jax.experimental import pallas as pl
from jax.experimental.pallas import tpu as pltpu
from jax.sharding import PartitionSpec as P

F32, BF16, I32 = jnp.float32, jnp.bfloat16, jnp.int32
NZ, NY, NC = 8, 4, 2
STEP = 256
SUB = 8
INFO = 8
MESH = pl.DeviceIdType.MESH
NN, NT = ((1,), (0,)), ((1,), (1,))


def split(value):
    high = value.astype(BF16)
    return high, (value - high.astype(F32)).astype(BF16)


def dot(lhs, rhs, contract):
    return lax.dot_general(lhs, rhs, (contract, ((), ())), preferred_element_type=F32)


def dot3(lh, ll, rh, rl, contract):
    return dot(lh, rh, contract) + (dot(lh, rl, contract) + dot(ll, rh, contract))


def chunk(c, step=STEP):
    return pl.ds(pl.multiple_of(c * step, step), step)


def ring(i, n):
    return lax.rem(i + 2 * n, n)


class Chain:
    def __init__(self, me, size, sign, length, piece, landing, send_sem, recv_sem, to):
        self.me, self.size, self.sign, self.length = me, size, sign, length
        self.piece, self.landing, self.send_sem, self.recv_sem, self.to = piece, landing, send_sem, recv_sem, to

    def owner(self, j):
        return ring(self.me + self.sign * (self.length - j), self.size)

    def copy(self, j):
        return pltpu.make_async_remote_copy(
            src_ref=self.piece(self.owner(j)),
            dst_ref=self.landing.at[j],
            send_sem=self.send_sem.at[j],
            recv_sem=self.recv_sem.at[j],
            device_id=self.to(ring(self.me + self.sign, self.size)),
            device_id_type=MESH,
        )

    def start(self):
        if self.length:
            self.copy(0).start()

    def advance(self, j):
        if j < self.length - 1:
            self.copy(j).wait_recv()
            here = self.piece(self.owner(j + 1))
            here[...] = here[...] + self.landing[j]
            self.copy(j + 1).start()

    def arrive(self, total):
        if not self.length:
            return total
        self.copy(self.length - 1).wait_recv()
        return total + self.landing[self.length - 1]

    def drain(self):
        for j in range(self.length):
            self.copy(j).wait_send()


def lengths(n):
    far, near = n // 2, n - 1 - n // 2
    return ((far, near), (near, far))


def pack_coef(occ_ref, vir_ref, coef_ref):
    n_occ, n_vir = occ_ref.shape[0], vir_ref.shape[1]
    width = n_vir + n_occ
    coef_ref[:n_vir], coef_ref[width : width + n_vir] = split(vir_ref[...].T)
    coef_ref[n_vir:width], coef_ref[width + n_vir :] = split(occ_ref[...])


def table_part(info_ref, g, first, coef_ref, tab_h, tab_l, n_occ, n_vir):
    nb = coef_ref.shape[1]
    width = n_vir + n_occ
    got = []
    for f in range(2):
        func = info_ref[g, first + f : first + f + 1, :]
        hot = lax.broadcasted_iota(I32, (nb, STEP), 0) == func
        hot = jnp.where(hot, 1.0, 0.0).astype(BF16)
        both = dot(coef_ref[...], hot, NN)
        got.append(both[:width] + both[width:])
    (vir_p, occ_p), (vir_q, occ_q) = [(v[:n_vir], v[n_vir:]) for v in got]
    cols = chunk(g)
    for i in range(n_occ):
        entry = occ_p[i : i + 1] * vir_q + occ_q[i : i + 1] * vir_p
        high, low = split(entry)
        tab_h[i * n_vir : (i + 1) * n_vir, cols] = high
        tab_l[i * n_vir : (i + 1) * n_vir, cols] = low


def build_matrix(info_ref, every, flip, mat_h, mat_l, tiles_dev):
    n_grp, per_dev, tile, _ = every.shape
    n_tiles = n_grp * tiles_dev
    for g in range(n_grp):
        for j in range(per_dev):
            flip[g, j] = every[g, j].T

    def body(step, carry):
        h, t = lax.div(step, n_tiles), lax.rem(step, n_tiles)
        dev_h, dev_t = lax.div(h, tiles_dev), lax.div(t, tiles_dev)
        total = jnp.zeros((tile, tile), F32)
        for j in range(per_dev):
            code = info_ref[dev_h, j : j + 1, :]
            here = jnp.logical_and(code[:, :tile] == h, code[:, tile:] == t)
            total = total + jnp.where(here, every[dev_h, j], 0.0)
            code = info_ref[dev_t, j : j + 1, :]
            here = jnp.logical_and(code[:, :tile] == t, code[:, tile:] == h)
            total = total + jnp.where(here, flip[dev_t, j], 0.0)
        high, low = split(total)
        mat_h[chunk(h, tile), chunk(t, tile)] = high
        mat_l[chunk(h, tile), chunk(t, tile)] = low
        return carry

    lax.fori_loop(0, n_tiles * n_tiles, body, 0)


def column_kernel(n_vir, tiles_dev, info_in, occ_ref, vir_ref, blocks_ref, half_out, orb_out,
                  infos, every, flip, coef_ref, tab_h, tab_l, mat_h, mat_l, g_h, g_l,
                  away, near, own, half, y1, z1, y2, z2,
                  info_s, info_r, block_s, block_r, core_s, core_r, half_s,
                  y1_s, y1_r, z1_s, z1_r, y2_s, y2_r, z2_s, z2_r):
    n_grp, per_dev = every.shape[:2]
    n_occ = occ_ref.shape[0]
    width, rows = tab_h.shape
    mine = width // n_grp
    grp, pair = lax.axis_index("grp"), lax.axis_index("pair")
    core = lax.rem(pair, NC)
    y = lax.rem(lax.div(pair, NC), NY)
    z = lax.div(pair, NC * NY)

    def at(z_, y_, core_):
        return (grp, (z_ * NY + y_) * NC + core_)

    peers = [(lax.rem(grp + d, n_grp), pair) for d in range(1, n_grp)]
    peers += [at(z, y, 1 - core)]
    peers += [at(z, ring(y + s, NY), core) for s in (1, -1)]
    peers += [at(ring(z + s, NZ), y, core) for s in (1, -1)]
    barrier = pltpu.get_barrier_semaphore()
    for peer in peers:
        pl.semaphore_signal(barrier, inc=1, device_id=peer, device_id_type=MESH)
    pack_coef(occ_ref, vir_ref, coef_ref)
    infos[grp] = info_in[...]
    pl.semaphore_wait(barrier, len(peers))

    def over_x(src, dst, d, send, recv):
        return pltpu.make_async_remote_copy(
            src_ref=src, dst_ref=dst.at[grp], send_sem=send.at[d], recv_sem=recv.at[d],
            device_id=(lax.rem(grp + d, n_grp), pair), device_id_type=MESH)

    for d in (1, 3, 2):
        over_x(info_in, infos, d, info_s, info_r).start()
    for d in (1, 3, 2):
        over_x(blocks_ref, every, d, block_s, block_r).start()
    mine_copy = pltpu.make_async_copy(blocks_ref, every.at[grp], block_r.at[0])
    mine_copy.start()

    def tables(d, carry):
        g = lax.rem(grp + n_grp - d, n_grp)

        @pl.when(d > 0)
        def _():
            over_x(info_in, infos, d, info_s, info_r).wait_recv()

        table_part(infos, g, per_dev, coef_ref, tab_h, tab_l, n_occ, n_vir)
        return carry

    lax.fori_loop(0, n_grp, tables, 0)
    mine_copy.wait()
    for d in range(1, n_grp):
        over_x(blocks_ref, every, d, block_s, block_r).wait_recv()
    build_matrix(infos, every, flip, mat_h, mat_l, tiles_dev)
    share = chunk(grp, mine)

    def make_g(c, carry):
        cols = chunk(c)
        g = dot3(tab_h[share, :], tab_l[share, :], mat_h[:, cols], mat_l[:, cols], NN)
        g = g.reshape(NZ * NY, NC, SUB, STEP)
        for k in range(NC):
            g_h[k, :, cols], g_l[k, :, cols] = split(g[:, k].reshape(NZ * NY * SUB, STEP))
        return carry

    lax.fori_loop(0, rows // STEP, make_g, 0)
    parts = width // STEP // 2

    def product(which, side, c):
        tab = chunk(side * parts + c)
        p = dot3(g_h[which], g_l[which], tab_h[tab, :], tab_l[tab, :], NT)
        return p.reshape(NZ, NY, SUB, STEP)

    def over_core(side, c):
        return pltpu.make_async_remote_copy(
            src_ref=away.at[side, c], dst_ref=near.at[side, c], send_sem=core_s.at[side, c],
            recv_sem=core_r.at[side, c], device_id=at(z, y, 1 - core), device_id_type=MESH)

    def sibling(side):
        def body(c, carry):
            away[side, c] = product(1 - core, side, c)
            over_core(side, c).start()
            return carry

        lax.fori_loop(0, parts, body, 0)

    def kept(side, lo, hi):
        def body(c, carry):
            p = product(core, side, c)
            over_core(side, c).wait_recv()
            own[side, c] = p + near[side, c]
            return carry

        lax.fori_loop(lo, hi, body, 0)

    def part(h):
        return slice(h * parts // 2, (h + 1) * parts // 2)

    def chains(size, me, piece, landing, send, recv, to):
        return [
            [Chain(me, size, (1, -1)[d], lengths(size)[h][d], functools.partial(piece, h), landing.at[h, d],
                   send.at[h, d], recv.at[h, d], to) for d in range(2)]
            for h in range(2)
        ]

    to_y, to_z = (lambda v: at(z, v, core)), (lambda v: at(v, y, core))
    on_y1 = chains(NY, y, lambda h, v: own.at[1, part(h), :, v], y1, y1_s, y1_r, to_y)
    on_z2 = chains(NZ, z, lambda h, v: own.at[1, part(h), v, y], z2, z2_s, z2_r, to_z)
    on_z1 = chains(NZ, z, lambda h, v: own.at[0, part(h), v], z1, z1_s, z1_r, to_z)
    on_y2 = chains(NY, y, lambda h, v: own.at[0, part(h), z, v], y2, y2_s, y2_r, to_y)

    def start(pair_):
        for chain in pair_:
            chain.start()

    def advance(group, j):
        for chain in [c for pair_ in group for c in pair_]:
            chain.advance(j)

    def arrive(pair_, here):
        total = here[...]
        for chain in pair_:
            total = chain.arrive(total)
        return total

    def finish(side, h, pair_):
        total = arrive(pair_, own.at[side, part(h), z, y])
        for j in range(parts // 2):
            first = (side * parts + h * parts // 2 + j) * STEP
            orb_out[:, first : first + STEP] = total[j]

    local = chunk(grp, tiles_dev * (rows // n_grp // tiles_dev))

    def half_copy(c):
        return pltpu.make_async_copy(half.at[:, chunk(c)], half_out.at[:, chunk(c)], half_s.at[c])

    def half_part(lo, hi):
        def body(c, carry):
            tab = chunk(c)
            half[:, tab] = dot3(mat_h[local, :], mat_l[local, :], tab_h[tab, :], tab_l[tab, :], NT)
            half_copy(c).start()
            return carry

        lax.fori_loop(lo, hi, body, 0)

    sibling(1)
    kept(1, 0, parts // 2)
    start(on_y1[0])
    kept(1, parts // 2, parts)
    start(on_y1[1])
    sibling(0)
    advance(on_y1, 0)
    kept(0, 0, parts // 2)
    start(on_z1[0])
    kept(0, parts // 2, parts)
    start(on_z1[1])
    for h in range(2):
        here = own.at[1, part(h), :, y]
        here[...] = arrive(on_y1[h], here)
        start(on_z2[h])
    for j in range(max(max(lengths(NZ)[0]) - 1, 0)):
        half_part(2 * j, 2 * j + 2)
        advance(on_z1, j)
        advance(on_z2, j)
    half_part(2 * max(max(lengths(NZ)[0]) - 1, 0), width // STEP)
    for h in range(2):
        here = own.at[0, part(h), z]
        here[...] = arrive(on_z1[h], here)
        start(on_y2[h])
    for h in range(2):
        finish(1, h, on_z2[h])
    for j in range(max(lengths(NY)[0]) - 1):
        advance(on_y2, j)
    for h in range(2):
        finish(0, h, on_y2[h])

    for d in range(1, n_grp):
        over_x(info_in, infos, d, info_s, info_r).wait_send()
        over_x(blocks_ref, every, d, block_s, block_r).wait_send()
    for group in (on_y1, on_z1, on_y2, on_z2):
        for pair_ in group:
            for chain in pair_:
                chain.drain()

    def settle(c, carry):
        for side in range(2):
            over_core(side, c).wait_send()
            half_copy(side * parts + c).wait()
        return carry

    lax.fori_loop(0, parts, settle, 0)


def on_device(blocks, block_home, block_group, block_slot, pair_funcs, occ_coef, vir_coef):
    n_grp = lax.axis_size("grp")
    grp = lax.axis_index("grp")
    per_dev, tile, _ = blocks.shape
    rows_dev = pair_funcs.shape[1]
    tiles_dev = rows_dev // tile
    nb, n_occ = occ_coef.shape
    n_vir = vir_coef.shape[1]
    width = n_occ * n_vir
    rows = rows_dev * n_grp
    kept = NZ * NY * SUB
    parts = width // STEP // 2
    codes = [grp * tiles_dev + block_home, block_group[:, 0] * tiles_dev + block_slot]
    codes = jnp.concatenate([jnp.broadcast_to(c[:, None], (per_dev, tile)) for c in codes], axis=1)
    info = jnp.concatenate([codes, pair_funcs, jnp.zeros((INFO - per_dev - 2, rows_dev), I32)], axis=0)
    vmem = pl.BlockSpec(memory_space=pltpu.VMEM)
    hbm = pl.BlockSpec(memory_space=pl.ANY)
    dma = pltpu.SemaphoreType.DMA
    zh, yh = max(NZ // 2, 1), max(NY // 2, 1)
    return pl.pallas_call(
        functools.partial(column_kernel, n_vir, tiles_dev),
        out_shape=(jax.ShapeDtypeStruct((rows_dev, width), F32), jax.ShapeDtypeStruct((SUB, width), F32)),
        in_specs=[vmem, vmem, vmem, hbm],
        out_specs=(hbm, vmem),
        scratch_shapes=[
            pltpu.VMEM((n_grp, INFO, rows_dev), I32),
            pltpu.VMEM((n_grp, per_dev, tile, tile), F32),
            pltpu.VMEM((n_grp, per_dev, tile, tile), F32),
            pltpu.VMEM((2 * (n_occ + n_vir), nb), BF16),
            pltpu.VMEM((width, rows), BF16),
            pltpu.VMEM((width, rows), BF16),
            pltpu.VMEM((rows, rows), BF16),
            pltpu.VMEM((rows, rows), BF16),
            pltpu.VMEM((NC, kept, rows), BF16),
            pltpu.VMEM((NC, kept, rows), BF16),
            pltpu.VMEM((2, parts, NZ, NY, SUB, STEP), F32),
            pltpu.VMEM((2, parts, NZ, NY, SUB, STEP), F32),
            pltpu.VMEM((2, parts, NZ, NY, SUB, STEP), F32),
            pltpu.VMEM((rows_dev, width), F32),
            pltpu.VMEM((2, 2, yh, parts // 2, NZ, SUB, STEP), F32),
            pltpu.VMEM((2, 2, zh, parts // 2, NY, SUB, STEP), F32),
            pltpu.VMEM((2, 2, yh, parts // 2, SUB, STEP), F32),
            pltpu.VMEM((2, 2, zh, parts // 2, SUB, STEP), F32),
            dma((n_grp,)), dma((n_grp,)), dma((n_grp,)), dma((n_grp,)),
            dma((2, parts)), dma((2, parts)), dma((2 * parts,)),
            dma((2, 2, yh)), dma((2, 2, yh)), dma((2, 2, zh)), dma((2, 2, zh)),
            dma((2, 2, yh)), dma((2, 2, yh)), dma((2, 2, zh)), dma((2, 2, zh)),
        ],
        compiler_params=pltpu.CompilerParams(
            collective_id=0, has_side_effects=True, vmem_limit_bytes=56 * 2**20
        ),
    )(info, occ_coef.T, vir_coef, blocks)


def solution(mesh):
    both = ("grp", "pair")
    placed = (P(both, None, None), P(both), P(both, None), P(both), P(None, both), P(), P())
    return jax.shard_map(
        on_device,
        mesh=mesh,
        in_specs=placed,
        out_specs=(P(both, None), P(both, None)),
        check_vma=False,
    )
```

```python
import functools

import jax
import jax.numpy as jnp
from jax import lax
from jax.experimental import pallas as pl
from jax.experimental.pallas import tpu as pltpu
from jax.sharding import PartitionSpec as P

F32, BF16, I32 = jnp.float32, jnp.bfloat16, jnp.int32
NZ, NY, NC = 8, 4, 2
STEP = 256
SUB = 8
INFO = 8
WIDE = 512
VMEM_MIB = 56
MESH = pl.DeviceIdType.MESH
NN, NT = ((1,), (0,)), ((1,), (1,))


def split(value):
    high = value.astype(BF16)
    return high, (value - high.astype(F32)).astype(BF16)


def dot(lhs, rhs, contract):
    return lax.dot_general(lhs, rhs, (contract, ((), ())), preferred_element_type=F32)


def dot3(lh, ll, rh, rl, contract):
    return dot(lh, rh, contract) + (dot(lh, rl, contract) + dot(ll, rh, contract))


def chunk(c, step=STEP):
    return pl.ds(pl.multiple_of(c * step, step), step)


def ring(i, n):
    return lax.rem(i + 2 * n, n)


class Chain:
    def __init__(self, me, size, sign, length, piece, landing, send_sem, recv_sem, to):
        self.me, self.size, self.sign, self.length = me, size, sign, length
        self.piece, self.landing, self.send_sem, self.recv_sem, self.to = piece, landing, send_sem, recv_sem, to

    def owner(self, j):
        return ring(self.me + self.sign * (self.length - j), self.size)

    def copy(self, j):
        return pltpu.make_async_remote_copy(
            src_ref=self.piece(self.owner(j)),
            dst_ref=self.landing.at[j],
            send_sem=self.send_sem.at[j],
            recv_sem=self.recv_sem.at[j],
            device_id=self.to(ring(self.me + self.sign, self.size)),
            device_id_type=MESH,
        )

    def start(self):
        if self.length:
            self.copy(0).start()

    def advance(self, j):
        if j < self.length - 1:
            self.copy(j).wait_recv()
            here = self.piece(self.owner(j + 1))
            here[...] = here[...] + self.landing[j]
            self.copy(j + 1).start()

    def arrive(self, total):
        if not self.length:
            return total
        self.copy(self.length - 1).wait_recv()
        return total + self.landing[self.length - 1]

    def drain(self):
        for j in range(self.length):
            self.copy(j).wait_send()


def lengths(n):
    far, near = n // 2, n - 1 - n // 2
    return ((far, near), (near, far))


def pack_coef(occ_ref, vir_ref, coef_ref):
    n_occ, n_vir = occ_ref.shape[0], vir_ref.shape[1]
    width = n_vir + n_occ
    coef_ref[:n_vir], coef_ref[width : width + n_vir] = split(vir_ref[...].T)
    coef_ref[n_vir:width], coef_ref[width + n_vir :] = split(occ_ref[...])


def table_part(info_ref, g, first, coef_ref, tab_h, tab_l, n_occ, n_vir):
    nb = coef_ref.shape[1]
    width = n_vir + n_occ
    got = []
    for f in range(2):
        func = info_ref[g, first + f : first + f + 1, :]
        hot = lax.broadcasted_iota(I32, (nb, STEP), 0) == func
        hot = jnp.where(hot, 1.0, 0.0).astype(BF16)
        both = dot(coef_ref[...], hot, NN)
        got.append(both[:width] + both[width:])
    (vir_p, occ_p), (vir_q, occ_q) = [(v[:n_vir], v[n_vir:]) for v in got]
    cols = chunk(g)
    for i in range(n_occ):
        entry = occ_p[i : i + 1] * vir_q + occ_q[i : i + 1] * vir_p
        high, low = split(entry)
        tab_h[i * n_vir : (i + 1) * n_vir, cols] = high
        tab_l[i * n_vir : (i + 1) * n_vir, cols] = low


def build_matrix(info_ref, every, flip, mat_h, mat_l, tiles_dev):
    n_grp, per_dev, tile, _ = every.shape
    n_tiles = n_grp * tiles_dev
    def body(step, carry):
        h, t = lax.div(step, n_tiles), lax.rem(step, n_tiles)
        dev_h, dev_t = lax.div(h, tiles_dev), lax.div(t, tiles_dev)
        total = jnp.zeros((tile, tile), F32)
        for j in range(per_dev):
            code = info_ref[dev_h, j : j + 1, :]
            here = jnp.logical_and(code[:, :tile] == h, code[:, tile:] == t)
            total = total + jnp.where(here, every[dev_h, j], 0.0)
            code = info_ref[dev_t, j : j + 1, :]
            here = jnp.logical_and(code[:, :tile] == t, code[:, tile:] == h)
            total = total + jnp.where(here, flip[dev_t, j], 0.0)
        high, low = split(total)
        mat_h[chunk(h, tile), chunk(t, tile)] = high
        mat_l[chunk(h, tile), chunk(t, tile)] = low
        return carry

    lax.fori_loop(0, n_tiles * n_tiles, body, 0)


class Direct:
    def __init__(self, me, size, piece, landing, send_sem, recv_sem, to):
        self.me, self.size, self.piece, self.landing = me, size, piece, landing
        self.send_sem, self.recv_sem, self.to = send_sem, recv_sem, to

    def copy(self, d):
        peer = ring(self.me + d, self.size)
        return pltpu.make_async_remote_copy(
            src_ref=self.piece(peer),
            dst_ref=self.landing.at[d],
            send_sem=self.send_sem.at[d],
            recv_sem=self.recv_sem.at[d],
            device_id=self.to(peer),
            device_id_type=MESH,
        )

    def order(self):
        return sorted(range(1, self.size), key=lambda d: -min(d, self.size - d))

    def start(self):
        for d in self.order():
            self.copy(d).start()

    def arrive(self, total):
        for d in reversed(self.order()):
            self.copy(d).wait_recv()
            total = total + self.landing[d]
        return total

    def drain(self):
        for d in range(1, self.size):
            self.copy(d).wait_send()


def column_kernel(n_vir, tiles_dev, home_in, group_in, slot_in, funcs_in, occ_in, vir_in, blocks_ref,
                  half_out, orb_out, home_ref, group_ref, slot_ref, funcs_ref, occ_ref, vir_ref, infos, every, flip, coef_ref, tab_h, tab_l, mat_h, mat_l, g_h, g_l,
                  away, near, own, half, y1, z1, y2, z2,
                  info_s, info_r, block_s, block_r, own_s, core_s, core_r, half_s,
                  y1_s, y1_r, z1_s, z1_r, y2_s, y2_r, z2_s, z2_r):
    n_grp, per_dev, tile, _ = every.shape
    n_occ = occ_ref.shape[0]
    width, rows = tab_h.shape
    mine = width // n_grp
    grp, pair = lax.axis_index("grp"), lax.axis_index("pair")
    core = lax.rem(pair, NC)
    y = lax.rem(lax.div(pair, NC), NY)
    z = lax.div(pair, NC * NY)
    right, left = ring(grp + 1, n_grp), ring(grp - 1, n_grp)
    far = ring(grp + 2, n_grp)

    def at(z_, y_, core_):
        return (grp, (z_ * NY + y_) * NC + core_)

    def to_y(v):
        return at(z, v, core)

    def to_z(v):
        return at(v, y, core)

    peers = [(ring(grp + d, n_grp), pair) for d in range(1, n_grp)]
    peers += [at(z, y, 1 - core)]
    peers += [to_y(ring(y + d, NY)) for d in range(1, NY)]
    peers += [to_z(ring(z + d, NZ)) for d in range(1, NZ)]
    pairs = ((home_in, home_ref), (group_in, group_ref), (slot_in, slot_ref), (funcs_in, funcs_ref),
             (occ_in, occ_ref), (vir_in, vir_ref))
    fetches = [pltpu.make_async_copy(src, dst, own_s.at[1 + i]) for i, (src, dst) in enumerate(pairs)]
    for fetch in fetches:
        fetch.start()
    barrier = pltpu.get_barrier_semaphore()
    for peer in peers:
        pl.semaphore_signal(barrier, inc=1, device_id=peer, device_id_type=MESH)
    for fetch in fetches[:4]:
        fetch.wait()
    lane = lax.broadcasted_iota(I32, (1, STEP), 1)
    for j in range(per_dev):
        home = grp * tiles_dev + home_ref[j]
        partner = group_ref[j] * tiles_dev + slot_ref[j]
        infos[grp, j : j + 1, :] = jnp.where(lane < tile, home, partner)
    infos[grp, per_dev : per_dev + 2, :] = funcs_ref[...]
    infos[grp, per_dev + 2 :, :] = jnp.zeros((INFO - per_dev - 2, STEP), I32)
    pl.semaphore_wait(barrier, len(peers))

    def tell(d):
        return pltpu.make_async_remote_copy(
            src_ref=infos.at[grp], dst_ref=infos.at[grp], send_sem=info_s.at[d], recv_sem=info_r.at[d],
            device_id=(ring(grp + d, n_grp), pair), device_id_type=MESH)

    split_at = per_dev // 2
    parts_of = (slice(0, split_at), slice(split_at, per_dev))

    def pass_on(way, step):
        to = (right, left)[way]
        which = parts_of[way if step != 1 else 1 - way]
        if step < 2:
            src, dst = blocks_ref.at[which], every.at[grp, which]
        else:
            src = dst = every.at[(left, right)[way], which]
        return pltpu.make_async_remote_copy(
            src_ref=src, dst_ref=dst, send_sem=block_s.at[way, step], recv_sem=block_r.at[way, step],
            device_id=(to, pair), device_id_type=MESH)

    for d in (1, 3, 2):
        tell(d).start()
    for step in range(2):
        for way in range(2):
            pass_on(way, step).start()
    mine_copy = pltpu.make_async_copy(blocks_ref, every.at[grp], own_s.at[0])
    mine_copy.start()
    for fetch in fetches[4:]:
        fetch.wait()
    pack_coef(occ_ref, vir_ref, coef_ref)

    def tables(d, carry):
        g = ring(grp - d, n_grp)

        @pl.when(d > 0)
        def _():
            tell(d).wait_recv()

        table_part(infos, g, per_dev, coef_ref, tab_h, tab_l, n_occ, n_vir)
        return carry

    lax.fori_loop(0, n_grp, tables, 0)
    for way in range(2):
        pass_on(way, 0).wait_recv()
        pass_on(way, 2).start()

    def turn(g, which):
        for j in range(which.start, which.stop):
            flip[g, j] = every[g, j].T

    mine_copy.wait()
    turn(grp, slice(0, per_dev))
    for way in range(2):
        pass_on(way, 1).wait_recv()
        turn((left, right)[way], slice(0, per_dev))
    for way in range(2):
        pass_on(way, 2).wait_recv()
        turn(far, parts_of[way])
    build_matrix(infos, every, flip, mat_h, mat_l, tiles_dev)
    share = chunk(grp, mine)

    def make_g(c, carry):
        cols = chunk(c, WIDE)
        g = dot3(tab_h[share, :], tab_l[share, :], mat_h[:, cols], mat_l[:, cols], NN)
        g = g.reshape(NZ * NY, NC, SUB, WIDE)
        for k in range(NC):
            kept = lax.rem(core + k + 1, NC)
            g_h[kept, :, cols], g_l[kept, :, cols] = split(g[:, k].reshape(NZ * NY * SUB, WIDE))
        return carry

    lax.fori_loop(0, rows // WIDE, make_g, 0)
    pieces = width // WIDE

    def over_core(p):
        return pltpu.make_async_remote_copy(
            src_ref=away.at[p], dst_ref=near.at[p], send_sem=core_s.at[p], recv_sem=core_r.at[p],
            device_id=at(z, y, 1 - core), device_id_type=MESH)

    def produce(p):
        tab = slice(p * WIDE, (p + 1) * WIDE)
        value = dot3(g_h[...].reshape(-1, rows), g_l[...].reshape(-1, rows), tab_h[tab, :], tab_l[tab, :], NT)
        value = value.reshape(NC, NZ, NY, SUB, WIDE)
        away[p] = value[0]
        own[p] = value[1]
        over_core(p).start()

    def settle(p):
        over_core(p).wait_recv()
        own[p] = own[p] + near[p]

    def chains(p, size, me, piece, landing, send, recv, to):
        hops = lengths(size)[p // 2 % 2]
        return [Chain(me, size, (1, -1)[d], hops[d], piece, landing.at[d], send.at[d], recv.at[d], to)
                for d in range(2)]

    first, second = [], []
    for p in range(pieces):
        i = p // 2
        if p % 2 == 0:
            first.append(chains(p, NZ, z, lambda v, p=p: own.at[p, v], z1.at[i], z1_s.at[i], z1_r.at[i], to_z))
            second.append([Direct(y, NY, lambda v, p=p: own.at[p, z, v], y2.at[i], y2_s.at[i], y2_r.at[i], to_y)])
        else:
            first.append(chains(p, NY, y, lambda v, p=p: own.at[p, :, v], y1.at[i], y1_s.at[i], y1_r.at[i], to_y))
            second.append([Direct(z, NZ, lambda v, p=p: own.at[p, v, y], z2.at[i], z2_s.at[i], z2_r.at[i], to_z)])

    def start(group):
        for way in group:
            way.start()

    def advance(p, j):
        for way in first[p]:
            way.advance(j)

    def turn_corner(p):
        here = own.at[p, z] if p % 2 == 0 else own.at[p, :, y]
        total = here[...]
        for way in first[p]:
            total = way.arrive(total)
        here[...] = total
        start(second[p])

    def finish(p):
        total = own[p, z, y]
        for way in second[p]:
            total = way.arrive(total)
        orb_out[:, p * WIDE : (p + 1) * WIDE] = total

    local = chunk(grp, rows // n_grp)

    def half_copy(c):
        cols = slice(c * WIDE, (c + 1) * WIDE)
        return pltpu.make_async_copy(half.at[:, cols], half_out.at[:, cols], half_s.at[c])

    def half_part(c):
        tab = slice(c * WIDE, (c + 1) * WIDE)
        half[:, tab] = dot3(mat_h[local, :], mat_l[local, :], tab_h[tab, :], tab_l[tab, :], NT)
        half_copy(c).start()

    produce(0)
    produce(1)
    settle(0)
    start(first[0])
    produce(2)
    settle(1)
    start(first[1])
    advance(0, 0)
    produce(3)
    settle(2)
    start(first[2])
    advance(1, 0)
    advance(0, 1)
    half_part(0)
    settle(3)
    start(first[3])
    half_part(1)
    advance(0, 2)
    advance(2, 0)
    half_part(2)
    turn_corner(1)
    advance(3, 0)
    advance(2, 1)
    half_part(3)
    turn_corner(0)
    advance(2, 2)
    turn_corner(3)
    turn_corner(2)
    for p in (1, 0, 3, 2):
        finish(p)

    for d in range(1, n_grp):
        tell(d).wait_send()
    for way in range(2):
        for step in range(3):
            pass_on(way, step).wait_send()
    for group in first + second:
        for way in group:
            way.drain()
    for p in range(pieces):
        over_core(p).wait_send()
        half_copy(p).wait()


def on_device(blocks, block_home, block_group, block_slot, pair_funcs, occ_coef, vir_coef):
    n_grp = lax.axis_size("grp")
    per_dev, tile, _ = blocks.shape
    rows_dev = pair_funcs.shape[1]
    tiles_dev = rows_dev // tile
    nb, n_occ = occ_coef.shape
    n_vir = vir_coef.shape[1]
    width = n_occ * n_vir
    rows = rows_dev * n_grp
    kept = NZ * NY * SUB
    pieces = width // WIDE
    vmem = pl.BlockSpec(memory_space=pltpu.VMEM)
    hbm = pl.BlockSpec(memory_space=pltpu.HBM)
    anywhere = pl.BlockSpec(memory_space=pl.ANY)
    dma = pltpu.SemaphoreType.DMA
    some = pieces // 2
    zh, yh = max(NZ // 2, 1), max(NY // 2, 1)
    return pl.pallas_call(
        functools.partial(column_kernel, n_vir, tiles_dev),
        out_shape=(jax.ShapeDtypeStruct((rows_dev, width), F32), jax.ShapeDtypeStruct((SUB, width), F32)),
        in_specs=[hbm] * 7,
        out_specs=(anywhere, vmem),
        scratch_shapes=[
            pltpu.SMEM((per_dev,), I32),
            pltpu.SMEM((per_dev,), I32),
            pltpu.SMEM((per_dev,), I32),
            pltpu.VMEM((2, rows_dev), I32),
            pltpu.VMEM((n_occ, nb), F32),
            pltpu.VMEM((nb, n_vir), F32),
            pltpu.VMEM((n_grp, INFO, rows_dev), I32),
            pltpu.VMEM((n_grp, per_dev, tile, tile), F32),
            pltpu.VMEM((n_grp, per_dev, tile, tile), F32),
            pltpu.VMEM((2 * (n_occ + n_vir), nb), BF16),
            pltpu.VMEM((width, rows), BF16),
            pltpu.VMEM((width, rows), BF16),
            pltpu.VMEM((rows, rows), BF16),
            pltpu.VMEM((rows, rows), BF16),
            pltpu.VMEM((NC, kept, rows), BF16),
            pltpu.VMEM((NC, kept, rows), BF16),
            pltpu.VMEM((pieces, NZ, NY, SUB, WIDE), F32),
            pltpu.VMEM((pieces, NZ, NY, SUB, WIDE), F32),
            pltpu.VMEM((pieces, NZ, NY, SUB, WIDE), F32),
            pltpu.VMEM((rows_dev, width), F32),
            pltpu.VMEM((some, 2, yh, NZ, SUB, WIDE), F32),
            pltpu.VMEM((some, 2, zh, NY, SUB, WIDE), F32),
            pltpu.VMEM((some, NY, SUB, WIDE), F32),
            pltpu.VMEM((some, NZ, SUB, WIDE), F32),
            dma((n_grp,)), dma((n_grp,)), dma((2, 3)), dma((2, 3)), dma((7,)),
            dma((pieces,)), dma((pieces,)), dma((pieces,)),
            dma((some, 2, yh)), dma((some, 2, yh)), dma((some, 2, zh)), dma((some, 2, zh)),
            dma((some, NY)), dma((some, NY)), dma((some, NZ)), dma((some, NZ)),
        ],
        compiler_params=pltpu.CompilerParams(
            collective_id=0, has_side_effects=True, vmem_limit_bytes=VMEM_MIB * 2**20
        ),
    )(block_home, block_group.reshape(per_dev), block_slot, pair_funcs, occ_coef.T, vir_coef, blocks)


def solution(mesh):
    both = ("grp", "pair")
    placed = (P(both, None, None), P(both), P(both, None), P(both), P(None, both), P(), P())
    return jax.shard_map(
        on_device,
        mesh=mesh,
        in_specs=placed,
        out_specs=(P(both, None), P(both, None)),
        check_vma=False,
    )
```

```python
import functools

import jax
import jax.numpy as jnp
from jax import lax
from jax.experimental import pallas as pl
from jax.experimental.pallas import tpu as pltpu
from jax.sharding import PartitionSpec as P

F32, BF16, I32 = jnp.float32, jnp.bfloat16, jnp.int32
NZ, NY, NC = 8, 4, 2
STEP = 256
SUB = 8
INFO = 8
WIDE = 256
OWN = 1
HALVES = 4
VMEM_MIB = 56
MESH = pl.DeviceIdType.MESH
NN, NT = ((1,), (0,)), ((1,), (1,))


def split(value):
    high = value.astype(BF16)
    return high, (value - high.astype(F32)).astype(BF16)


def dot(lhs, rhs, contract):
    return lax.dot_general(lhs, rhs, (contract, ((), ())), preferred_element_type=F32)


def dot3(lh, ll, rh, rl, contract):
    return dot(lh, rh, contract) + (dot(lh, rl, contract) + dot(ll, rh, contract))


def chunk(c, step=STEP):
    return pl.ds(pl.multiple_of(c * step, step), step)


def ring(i, n):
    return lax.rem(i + 2 * n, n)


class Chain:
    def __init__(self, me, size, sign, length, piece, landing, send_sem, recv_sem, to):
        self.me, self.size, self.sign, self.length = me, size, sign, length
        self.piece, self.landing, self.send_sem, self.recv_sem, self.to = piece, landing, send_sem, recv_sem, to

    def owner(self, j):
        return ring(self.me + self.sign * (self.length - j), self.size)

    def copy(self, j):
        return pltpu.make_async_remote_copy(
            src_ref=self.piece(self.owner(j)),
            dst_ref=self.landing.at[j],
            send_sem=self.send_sem.at[j],
            recv_sem=self.recv_sem.at[j],
            device_id=self.to(ring(self.me + self.sign, self.size)),
            device_id_type=MESH,
        )

    def start(self):
        if self.length:
            self.copy(0).start()

    def advance(self, j):
        if j < self.length - 1:
            self.copy(j).wait_recv()
            here = self.piece(self.owner(j + 1))
            here[...] = here[...] + self.landing[j]
            self.copy(j + 1).start()

    def arrive(self, total):
        if not self.length:
            return total
        self.copy(self.length - 1).wait_recv()
        return total + self.landing[self.length - 1]

    def drain(self):
        for j in range(self.length):
            self.copy(j).wait_send()


def lengths(n):
    far, near = n // 2, n - 1 - n // 2
    return ((far, near), (near, far))


def pack_coef(occ_ref, vir_ref, coef_ref):
    n_occ, n_vir = occ_ref.shape[0], vir_ref.shape[1]
    width = n_vir + n_occ
    coef_ref[:n_vir], coef_ref[width : width + n_vir] = split(vir_ref[...].T)
    coef_ref[n_vir:width], coef_ref[width + n_vir :] = split(occ_ref[...])


def table_part(info_ref, g, first, coef_ref, tab_h, tab_l, n_occ, n_vir):
    nb = coef_ref.shape[1]
    width = n_vir + n_occ
    got = []
    for f in range(2):
        func = info_ref[g, first + f : first + f + 1, :]
        hot = lax.broadcasted_iota(I32, (nb, STEP), 0) == func
        hot = jnp.where(hot, 1.0, 0.0).astype(BF16)
        both = dot(coef_ref[...], hot, NN)
        got.append(both[:width] + both[width:])
    (vir_p, occ_p), (vir_q, occ_q) = [(v[:n_vir], v[n_vir:]) for v in got]
    cols = chunk(g)
    for i in range(n_occ):
        entry = occ_p[i : i + 1] * vir_q + occ_q[i : i + 1] * vir_p
        high, low = split(entry)
        tab_h[i * n_vir : (i + 1) * n_vir, cols] = high
        tab_l[i * n_vir : (i + 1) * n_vir, cols] = low


def build_tile(info_ref, every, flip, mat_h, mat_l, tiles_dev, group_of, h, t):
    _, per_dev, tile, _ = every.shape
    dev_h, dev_t = lax.div(h, tiles_dev), lax.div(t, tiles_dev)
    tile_h = group_of(dev_h) * tiles_dev + lax.rem(h, tiles_dev)
    tile_t = group_of(dev_t) * tiles_dev + lax.rem(t, tiles_dev)
    total = jnp.zeros((tile, tile), F32)
    for j in range(per_dev):
        code = info_ref[dev_h, j : j + 1, :]
        here = jnp.logical_and(code[:, :tile] == tile_h, code[:, tile:] == tile_t)
        total = total + jnp.where(here, every[dev_h, j], 0.0)
        code = info_ref[dev_t, j : j + 1, :]
        here = jnp.logical_and(code[:, :tile] == tile_t, code[:, tile:] == tile_h)
        total = total + jnp.where(here, flip[dev_t, j], 0.0)
    high, low = split(total)
    mat_h[chunk(h, tile), chunk(t, tile)] = high
    mat_l[chunk(h, tile), chunk(t, tile)] = low


class Direct:
    def __init__(self, me, size, piece, landing, send_sem, recv_sem, to):
        self.me, self.size, self.piece, self.landing = me, size, piece, landing
        self.send_sem, self.recv_sem, self.to = send_sem, recv_sem, to

    def copy(self, d):
        peer = ring(self.me + d, self.size)
        return pltpu.make_async_remote_copy(
            src_ref=self.piece(peer),
            dst_ref=self.landing.at[d],
            send_sem=self.send_sem.at[d],
            recv_sem=self.recv_sem.at[d],
            device_id=self.to(peer),
            device_id_type=MESH,
        )

    def order(self):
        return sorted(range(1, self.size), key=lambda d: -min(d, self.size - d))

    def start(self):
        for d in self.order():
            self.copy(d).start()

    def arrive(self, total):
        for d in reversed(self.order()):
            self.copy(d).wait_recv()
            total = total + self.landing[d]
        return total

    def drain(self):
        for d in range(1, self.size):
            self.copy(d).wait_send()


def column_kernel(n_vir, tiles_dev, home_in, group_in, slot_in, funcs_in, occ_in, vir_in, blocks_ref,
                  half_out, orb_out, home_ref, group_ref, slot_ref, funcs_ref, occ_ref, vir_ref, infos, every, flip, coef_ref, tab_h, tab_l, mat_h, mat_l, g_sum, g_h, g_l,
                  away, near, own_z, own_y, half, y1, z1, y2, z2, zc,
                  info_s, info_r, block_s, block_r, own_s, core_s, core_r, half_s,
                  y1_s, y1_r, z1_s, z1_r, y2_s, y2_r, z2_s, z2_r, zc_s, zc_r):
    n_grp, per_dev, tile, _ = every.shape
    n_occ = occ_ref.shape[0]
    width, rows = tab_h.shape
    mine = width // n_grp
    grp, pair = lax.axis_index("grp"), lax.axis_index("pair")
    core = lax.rem(pair, NC)
    y = lax.rem(lax.div(pair, NC), NY)
    z = lax.div(pair, NC * NY)
    right, left = ring(grp + 1, n_grp), ring(grp - 1, n_grp)

    def group_of(slot):
        return ring(grp + OWN - slot, n_grp)

    def at(z_, y_, core_):
        return (grp, (z_ * NY + y_) * NC + core_)

    def to_y(v):
        return at(z, v, core)

    def to_z(v):
        return at(v, y, core)

    peers = [(ring(grp + d, n_grp), pair) for d in range(1, n_grp)]
    peers += [at(z, y, 1 - core)]
    peers += [to_y(ring(y + d, NY)) for d in range(1, NY)]
    peers += [to_z(ring(z + d, NZ)) for d in range(1, NZ)]
    pairs = ((home_in, home_ref), (group_in, group_ref), (slot_in, slot_ref), (funcs_in, funcs_ref),
             (occ_in, occ_ref), (vir_in, vir_ref))
    fetches = [pltpu.make_async_copy(src, dst, own_s.at[1 + i]) for i, (src, dst) in enumerate(pairs)]
    for fetch in fetches:
        fetch.start()
    barrier = pltpu.get_barrier_semaphore()
    for peer in peers:
        pl.semaphore_signal(barrier, inc=1, device_id=peer, device_id_type=MESH)
    for fetch in fetches[:4]:
        fetch.wait()
    lane = lax.broadcasted_iota(I32, (1, STEP), 1)
    for j in range(per_dev):
        home = grp * tiles_dev + home_ref[j]
        partner = group_ref[j] * tiles_dev + slot_ref[j]
        infos[OWN, j : j + 1, :] = jnp.where(lane < tile, home, partner)
    infos[OWN, per_dev : per_dev + 2, :] = funcs_ref[...]
    infos[OWN, per_dev + 2 :, :] = jnp.zeros((INFO - per_dev - 2, STEP), I32)
    pl.semaphore_wait(barrier, len(peers))

    def tell(d):
        return pltpu.make_async_remote_copy(
            src_ref=infos.at[OWN], dst_ref=infos.at[ring(OWN + d, n_grp)], send_sem=info_s.at[d], recv_sem=info_r.at[d],
            device_id=(ring(grp + d, n_grp), pair), device_id_type=MESH)

    split_at = per_dev // 2
    parts_of = (slice(0, split_at), slice(split_at, per_dev))

    def pass_on(way, step):
        to = (right, left)[way]
        which = parts_of[way if step != 1 else 1 - way]
        if step < 2:
            src, dst = blocks_ref.at[which], every.at[(OWN + 1, OWN - 1)[way], which]
        else:
            src, dst = every.at[(OWN + 1, OWN - 1)[way], which], every.at[OWN + 2, which]
        return pltpu.make_async_remote_copy(
            src_ref=src, dst_ref=dst, send_sem=block_s.at[way, step], recv_sem=block_r.at[way, step],
            device_id=(to, pair), device_id_type=MESH)

    for d in (1, 3, 2):
        tell(d).start()
    for step in range(2):
        for way in range(2):
            pass_on(way, step).start()
    mine_copy = pltpu.make_async_copy(blocks_ref, every.at[OWN], own_s.at[0])
    mine_copy.start()
    for fetch in fetches[4:]:
        fetch.wait()
    pack_coef(occ_ref, vir_ref, coef_ref)

    def tables(d, carry):
        slot = ring(OWN + d, n_grp)

        @pl.when(d > 0)
        def _():
            tell(d).wait_recv()

        table_part(infos, slot, per_dev, coef_ref, tab_h, tab_l, n_occ, n_vir)
        return carry

    lax.fori_loop(0, n_grp, tables, 0)
    for way in range(2):
        pass_on(way, 0).wait_recv()
        pass_on(way, 2).start()

    def turn(g, which):
        for j in range(which.start, which.stop):
            flip[g, j] = every[g, j].T

    n_tiles = rows // tile
    close = (OWN + 2) * tiles_dev
    rest = slice(close * tile, rows)
    share = chunk(grp, mine)

    def build(count_t, first_h, first_t):
        def body(step, carry):
            h, t = first_h + lax.div(step, count_t), first_t + lax.rem(step, count_t)
            build_tile(infos, every, flip, mat_h, mat_l, tiles_dev, group_of, h, t)
            return carry

        return body

    mine_copy.wait()
    turn(OWN, slice(0, per_dev))
    for way in range(2):
        pass_on(way, 1).wait_recv()
        turn((OWN + 1, OWN - 1)[way], slice(0, per_dev))
    lax.fori_loop(0, close * close, build(close, 0, 0), 0)

    def first_g(c, carry):
        cols = chunk(c)
        g_sum[:, cols] = dot3(tab_h[share, : close * tile], tab_l[share, : close * tile],
                              mat_h[: close * tile, cols], mat_l[: close * tile, cols], NN)
        return carry

    lax.fori_loop(0, close * tile // STEP, first_g, 0)

    def keep_g(g, cols):
        g = g.reshape(NZ * NY, NC, SUB, STEP)
        for k in range(NC):
            kept = lax.rem(core + k + 1, NC)
            g_h[kept, :, cols], g_l[kept, :, cols] = split(g[:, k].reshape(NZ * NY * SUB, STEP))

    for way in range(2):
        pass_on(way, 2).wait_recv()
        turn(OWN + 2, parts_of[way])
    lax.fori_loop(0, (n_tiles - close) * n_tiles, build(n_tiles, close, 0), 0)
    lax.fori_loop(0, close * (n_tiles - close), build(n_tiles - close, 0, close), 0)

    def second_g(c, carry):
        cols = chunk(c)
        keep_g(g_sum[:, cols] + dot3(tab_h[share, rest], tab_l[share, rest], mat_h[rest, cols], mat_l[rest, cols], NN), cols)
        return carry

    lax.fori_loop(0, close * tile // STEP, second_g, 0)
    keep_g(dot3(tab_h[share, :], tab_l[share, :], mat_h[:, rest], mat_l[:, rest], NN), rest)

    def over_core(p):
        return pltpu.make_async_remote_copy(
            src_ref=away.at[p], dst_ref=near.at[p], send_sem=core_s.at[p], recv_sem=core_r.at[p],
            device_id=at(z, y, 1 - core), device_id_type=MESH)

    pieces = width // WIDE
    some = pieces // 2

    def produce(p, own_ref, i):
        tab = chunk(p)
        value = dot3(g_h[...].reshape(-1, rows), g_l[...].reshape(-1, rows), tab_h[tab, :], tab_l[tab, :], NT)
        value = value.reshape(NC, NZ, NY, SUB, WIDE)
        away[p] = value[0]
        own_ref[i] = value[1]
        over_core(p).start()

    def settle(p, own_ref, i):
        over_core(p).wait_recv()
        own_ref[i] = own_ref[i] + near[p]

    def both_ways(i, size, me, piece, landing, send, recv, to):
        side = 1 - 2 * lax.rem(i, 2) if isinstance(i, jax.Array) else 1 - 2 * (i % 2)
        return [Chain(me, size, side * (1, -1)[d], lengths(size)[0][d], piece, landing.at[i, d], send.at[i, d],
                      recv.at[i, d], to) for d in range(2)]

    def round_z(i):
        return both_ways(i, NZ, z, lambda v: own_z.at[i, v], z1, z1_s, z1_r, to_z)

    def round_y(i):
        return both_ways(i, NY, y, lambda v: own_y.at[i, :, v], y1, y1_s, y1_r, to_y)

    def start(group):
        for way in group:
            way.start()

    def advance(group, j):
        for way in group:
            way.advance(j)

    def arrive(group, total):
        for way in group:
            total = way.arrive(total)
        return total

    def end_z(i):
        own_z[i, z] = arrive(round_z(i), own_z[i, z])

    def end_y(i):
        own_y[i, :, y] = arrive(round_y(i), own_y[i, :, y])

    def two(b):
        return slice(2 * b, 2 * b + 2)

    last_y = [Direct(y, NY, lambda v, b=b: own_z.at[two(b), z, v], y2.at[b], y2_s.at[b], y2_r.at[b], to_y)
              for b in range(some // 2)]
    last_z = Direct(z, NZ, lambda v: own_y.at[two(1), v, y], z2, z2_s, z2_r, to_z)
    chain_z = [Chain(z, NZ, (1, -1)[d], lengths(NZ)[0][d], lambda v: own_y.at[two(0), v, y], zc.at[d], zc_s.at[d],
                     zc_r.at[d], to_z) for d in range(2)]

    def give(side, b, group):
        total = arrive(group, (own_z, own_y)[side][two(b), z, y])
        for i in range(2):
            first = (2 * (2 * b + i) + side) * WIDE
            orb_out[:, first : first + WIDE] = total[i]

    local = slice(OWN * (rows // n_grp), (OWN + 1) * (rows // n_grp))
    wide = width // HALVES

    def half_copy(c):
        cols = slice(c * wide, (c + 1) * wide)
        return pltpu.make_async_copy(half.at[:, cols], half_out.at[:, cols], half_s.at[c])

    def half_part(c):
        tab = slice(c * wide, (c + 1) * wide)
        half[:, tab] = dot3(mat_h[local, :], mat_l[local, :], tab_h[tab, :], tab_l[tab, :], NT)
        half_copy(c).start()

    def steps(q, carry):
        produce(2 * q, own_z, q)

        @pl.when(q >= 1)
        def _():
            settle(2 * q - 1, own_y, q - 1)
            start(round_y(q - 1))

        produce(2 * q + 1, own_y, q)
        settle(2 * q, own_z, q)
        start(round_z(q))

        @pl.when(q >= 1)
        def _():
            advance(round_z(q - 1), 0)

        @pl.when(q >= 2)
        def _():
            advance(round_y(q - 2), 0)
            advance(round_z(q - 2), 1)

        @pl.when(q >= 3)
        def _():
            advance(round_z(q - 3), 2)

        return carry

    lax.fori_loop(0, some, steps, 0)
    settle(pieces - 1, own_y, 3)
    start(round_y(3))
    half_part(0)
    advance(round_y(2), 0)
    advance(round_z(3), 0)
    advance(round_z(2), 1)
    advance(round_z(1), 2)
    end_y(0)
    half_part(1)
    end_z(0)
    end_y(1)
    start(chain_z)
    advance(round_y(3), 0)
    advance(round_z(3), 1)
    advance(round_z(2), 2)
    end_z(1)
    last_y[0].start()
    end_y(2)
    advance(chain_z, 0)
    half_part(2)
    end_y(3)
    last_z.start()
    advance(round_z(3), 2)
    advance(chain_z, 1)
    end_z(2)
    half_part(3)
    advance(chain_z, 2)
    end_z(3)
    last_y[1].start()
    give(0, 0, last_y[:1])
    give(1, 0, chain_z)
    give(1, 1, [last_z])
    give(0, 1, last_y[1:])

    for d in range(1, n_grp):
        tell(d).wait_send()
    for way in range(2):
        for step in range(3):
            pass_on(way, step).wait_send()
    for way in last_y + [last_z] + chain_z:
        way.drain()
    for c in range(HALVES):
        half_copy(c).wait()

    def drain(i, carry):
        for way in round_z(i) + round_y(i):
            way.drain()
        for p in (2 * i, 2 * i + 1):
            over_core(p).wait_send()
        return carry

    lax.fori_loop(0, some, drain, 0)


def on_device(blocks, block_home, block_group, block_slot, pair_funcs, occ_coef, vir_coef):
    n_grp = lax.axis_size("grp")
    per_dev, tile, _ = blocks.shape
    rows_dev = pair_funcs.shape[1]
    tiles_dev = rows_dev // tile
    nb, n_occ = occ_coef.shape
    n_vir = vir_coef.shape[1]
    width = n_occ * n_vir
    rows = rows_dev * n_grp
    kept = NZ * NY * SUB
    pieces = width // WIDE
    vmem = pl.BlockSpec(memory_space=pltpu.VMEM)
    hbm = pl.BlockSpec(memory_space=pltpu.HBM)
    anywhere = pl.BlockSpec(memory_space=pl.ANY)
    dma = pltpu.SemaphoreType.DMA
    some = pieces // 2
    zh, yh = max(NZ // 2, 1), max(NY // 2, 1)
    return pl.pallas_call(
        functools.partial(column_kernel, n_vir, tiles_dev),
        out_shape=(jax.ShapeDtypeStruct((rows_dev, width), F32), jax.ShapeDtypeStruct((SUB, width), F32)),
        in_specs=[hbm] * 7,
        out_specs=(anywhere, vmem),
        scratch_shapes=[
            pltpu.SMEM((per_dev,), I32),
            pltpu.SMEM((per_dev,), I32),
            pltpu.SMEM((per_dev,), I32),
            pltpu.VMEM((2, rows_dev), I32),
            pltpu.VMEM((n_occ, nb), F32),
            pltpu.VMEM((nb, n_vir), F32),
            pltpu.VMEM((n_grp, INFO, rows_dev), I32),
            pltpu.VMEM((n_grp, per_dev, tile, tile), F32),
            pltpu.VMEM((n_grp, per_dev, tile, tile), F32),
            pltpu.VMEM((2 * (n_occ + n_vir), nb), BF16),
            pltpu.VMEM((width, rows), BF16),
            pltpu.VMEM((width, rows), BF16),
            pltpu.VMEM((rows, rows), BF16),
            pltpu.VMEM((rows, rows), BF16),
            pltpu.VMEM((width // n_grp, rows), F32),
            pltpu.VMEM((NC, kept, rows), BF16),
            pltpu.VMEM((NC, kept, rows), BF16),
            pltpu.VMEM((pieces, NZ, NY, SUB, WIDE), F32),
            pltpu.VMEM((pieces, NZ, NY, SUB, WIDE), F32),
            pltpu.VMEM((some, NZ, NY, SUB, WIDE), F32),
            pltpu.VMEM((some, NZ, NY, SUB, WIDE), F32),
            pltpu.VMEM((rows_dev, width), F32),
            pltpu.VMEM((some, 2, yh, NZ, SUB, WIDE), F32),
            pltpu.VMEM((some, 2, zh, NY, SUB, WIDE), F32),
            pltpu.VMEM((some // 2, NY, 2, SUB, WIDE), F32),
            pltpu.VMEM((NZ, 2, SUB, WIDE), F32),
            pltpu.VMEM((2, zh, 2, SUB, WIDE), F32),
            dma((n_grp,)), dma((n_grp,)), dma((2, 3)), dma((2, 3)), dma((7,)),
            dma((pieces,)), dma((pieces,)), dma((HALVES,)),
            dma((some, 2, yh)), dma((some, 2, yh)), dma((some, 2, zh)), dma((some, 2, zh)),
            dma((some // 2, NY)), dma((some // 2, NY)), dma((NZ,)), dma((NZ,)), dma((2, zh)), dma((2, zh)),
        ],
        compiler_params=pltpu.CompilerParams(
            collective_id=0, has_side_effects=True, vmem_limit_bytes=VMEM_MIB * 2**20
        ),
    )(block_home, block_group.reshape(per_dev), block_slot, pair_funcs, occ_coef.T, vir_coef, blocks)


def solution(mesh):
    both = ("grp", "pair")
    placed = (P(both, None, None), P(both), P(both, None), P(both), P(None, both), P(), P())
    return jax.shard_map(
        on_device,
        mesh=mesh,
        in_specs=placed,
        out_specs=(P(both, None), P(both, None)),
        check_vma=False,
    )
```

```python
import functools

import jax
import jax.numpy as jnp
from jax import lax
from jax.experimental import pallas as pl
from jax.experimental.pallas import tpu as pltpu
from jax.sharding import PartitionSpec as P

F32, BF16, I32 = jnp.float32, jnp.bfloat16, jnp.int32
NZ, NY, NC = 8, 4, 2
STEP = 256
SUB = 8
INFO = 8
WIDE = 512
VMEM_MIB = 56
MESH = pl.DeviceIdType.MESH
NN, NT = ((1,), (0,)), ((1,), (1,))


def split(value):
    high = value.astype(BF16)
    return high, (value - high.astype(F32)).astype(BF16)


def dot(lhs, rhs, contract):
    return lax.dot_general(lhs, rhs, (contract, ((), ())), preferred_element_type=F32)


def dot3(lh, ll, rh, rl, contract):
    return dot(lh, rh, contract) + (dot(lh, rl, contract) + dot(ll, rh, contract))


def chunk(c, step=STEP):
    return pl.ds(pl.multiple_of(c * step, step), step)


def ring(i, n):
    return lax.rem(i + 2 * n, n)


class Chain:
    def __init__(self, me, size, sign, length, piece, landing, send_sem, recv_sem, to):
        self.me, self.size, self.sign, self.length = me, size, sign, length
        self.piece, self.landing, self.send_sem, self.recv_sem, self.to = piece, landing, send_sem, recv_sem, to

    def owner(self, j):
        return ring(self.me + self.sign * (self.length - j), self.size)

    def copy(self, j):
        return pltpu.make_async_remote_copy(
            src_ref=self.piece(self.owner(j)),
            dst_ref=self.landing.at[j],
            send_sem=self.send_sem.at[j],
            recv_sem=self.recv_sem.at[j],
            device_id=self.to(ring(self.me + self.sign, self.size)),
            device_id_type=MESH,
        )

    def start(self):
        if self.length:
            self.copy(0).start()

    def advance(self, j):
        if j < self.length - 1:
            self.copy(j).wait_recv()
            here = self.piece(self.owner(j + 1))
            here[...] = here[...] + self.landing[j]
            self.copy(j + 1).start()

    def arrive(self, total):
        if not self.length:
            return total
        self.copy(self.length - 1).wait_recv()
        return total + self.landing[self.length - 1]

    def drain(self):
        for j in range(self.length):
            self.copy(j).wait_send()


def lengths(n):
    far, near = n // 2, n - 1 - n // 2
    return ((far, near), (near, far))


def pack_coef(occ_ref, vir_ref, coef_ref):
    n_occ, n_vir = occ_ref.shape[0], vir_ref.shape[1]
    width = n_vir + n_occ
    coef_ref[:n_vir], coef_ref[width : width + n_vir] = split(vir_ref[...].T)
    coef_ref[n_vir:width], coef_ref[width + n_vir :] = split(occ_ref[...])


def table_part(info_ref, g, first, coef_ref, tab_h, tab_l, n_occ, n_vir):
    nb = coef_ref.shape[1]
    width = n_vir + n_occ
    got = []
    for f in range(2):
        func = info_ref[g, first + f : first + f + 1, :]
        hot = lax.broadcasted_iota(I32, (nb, STEP), 0) == func
        hot = jnp.where(hot, 1.0, 0.0).astype(BF16)
        both = dot(coef_ref[...], hot, NN)
        got.append(both[:width] + both[width:])
    (vir_p, occ_p), (vir_q, occ_q) = [(v[:n_vir], v[n_vir:]) for v in got]
    cols = chunk(g)
    for i in range(n_occ):
        entry = occ_p[i : i + 1] * vir_q + occ_q[i : i + 1] * vir_p
        high, low = split(entry)
        tab_h[i * n_vir : (i + 1) * n_vir, cols] = high
        tab_l[i * n_vir : (i + 1) * n_vir, cols] = low


def build_matrix(info_ref, every, flip, mat_h, mat_l, tiles_dev):
    n_grp, per_dev, tile, _ = every.shape
    n_tiles = n_grp * tiles_dev
    def body(step, carry):
        h, t = lax.div(step, n_tiles), lax.rem(step, n_tiles)
        dev_h, dev_t = lax.div(h, tiles_dev), lax.div(t, tiles_dev)
        total = jnp.zeros((tile, tile), F32)
        for j in range(per_dev):
            code = info_ref[dev_h, j : j + 1, :]
            here = jnp.logical_and(code[:, :tile] == h, code[:, tile:] == t)
            total = total + jnp.where(here, every[dev_h, j], 0.0)
            code = info_ref[dev_t, j : j + 1, :]
            here = jnp.logical_and(code[:, :tile] == t, code[:, tile:] == h)
            total = total + jnp.where(here, flip[dev_t, j], 0.0)
        high, low = split(total)
        mat_h[chunk(h, tile), chunk(t, tile)] = high
        mat_l[chunk(h, tile), chunk(t, tile)] = low
        return carry

    lax.fori_loop(0, n_tiles * n_tiles, body, 0)


class Direct:
    def __init__(self, me, size, piece, landing, send_sem, recv_sem, to):
        self.me, self.size, self.piece, self.landing = me, size, piece, landing
        self.send_sem, self.recv_sem, self.to = send_sem, recv_sem, to

    def copy(self, d):
        peer = ring(self.me + d, self.size)
        return pltpu.make_async_remote_copy(
            src_ref=self.piece(peer),
            dst_ref=self.landing.at[d],
            send_sem=self.send_sem.at[d],
            recv_sem=self.recv_sem.at[d],
            device_id=self.to(peer),
            device_id_type=MESH,
        )

    def order(self):
        return sorted(range(1, self.size), key=lambda d: -min(d, self.size - d))

    def start(self):
        for d in self.order():
            self.copy(d).start()

    def arrive(self, total):
        for d in reversed(self.order()):
            self.copy(d).wait_recv()
            total = total + self.landing[d]
        return total

    def drain(self):
        for d in range(1, self.size):
            self.copy(d).wait_send()


def column_kernel(n_vir, tiles_dev, home_in, group_in, slot_in, funcs_in, occ_in, vir_in, blocks_ref,
                  half_out, orb_out, home_ref, group_ref, slot_ref, funcs_ref, occ_ref, vir_ref, infos, every, flip, coef_ref, tab_h, tab_l, mat_h, mat_l, g_h, g_l,
                  away, near, own, half, y1, z1, y2, z2, zc,
                  info_s, info_r, block_s, block_r, own_s, core_s, core_r, half_s,
                  y1_s, y1_r, z1_s, z1_r, y2_s, y2_r, z2_s, z2_r, zc_s, zc_r):
    n_grp, per_dev, tile, _ = every.shape
    n_occ = occ_ref.shape[0]
    width, rows = tab_h.shape
    mine = width // n_grp
    grp, pair = lax.axis_index("grp"), lax.axis_index("pair")
    core = lax.rem(pair, NC)
    y = lax.rem(lax.div(pair, NC), NY)
    z = lax.div(pair, NC * NY)
    right, left = ring(grp + 1, n_grp), ring(grp - 1, n_grp)
    far = ring(grp + 2, n_grp)

    def at(z_, y_, core_):
        return (grp, (z_ * NY + y_) * NC + core_)

    def to_y(v):
        return at(z, v, core)

    def to_z(v):
        return at(v, y, core)

    peers = [(ring(grp + d, n_grp), pair) for d in range(1, n_grp)]
    peers += [at(z, y, 1 - core)]
    peers += [to_y(ring(y + d, NY)) for d in range(1, NY)]
    peers += [to_z(ring(z + d, NZ)) for d in range(1, NZ)]
    pairs = ((home_in, home_ref), (group_in, group_ref), (slot_in, slot_ref), (funcs_in, funcs_ref),
             (occ_in, occ_ref), (vir_in, vir_ref))
    fetches = [pltpu.make_async_copy(src, dst, own_s.at[1 + i]) for i, (src, dst) in enumerate(pairs)]
    for fetch in fetches:
        fetch.start()
    barrier = pltpu.get_barrier_semaphore()
    for peer in peers:
        pl.semaphore_signal(barrier, inc=1, device_id=peer, device_id_type=MESH)
    for fetch in fetches[:4]:
        fetch.wait()
    lane = lax.broadcasted_iota(I32, (1, STEP), 1)
    for j in range(per_dev):
        home = grp * tiles_dev + home_ref[j]
        partner = group_ref[j] * tiles_dev + slot_ref[j]
        infos[grp, j : j + 1, :] = jnp.where(lane < tile, home, partner)
    infos[grp, per_dev : per_dev + 2, :] = funcs_ref[...]
    infos[grp, per_dev + 2 :, :] = jnp.zeros((INFO - per_dev - 2, STEP), I32)
    pl.semaphore_wait(barrier, len(peers))

    def tell(d):
        return pltpu.make_async_remote_copy(
            src_ref=infos.at[grp], dst_ref=infos.at[grp], send_sem=info_s.at[d], recv_sem=info_r.at[d],
            device_id=(ring(grp + d, n_grp), pair), device_id_type=MESH)

    split_at = per_dev // 2
    parts_of = (slice(0, split_at), slice(split_at, per_dev))

    def pass_on(way, step):
        to = (right, left)[way]
        which = parts_of[way if step != 1 else 1 - way]
        if step < 2:
            src, dst = blocks_ref.at[which], every.at[grp, which]
        else:
            src = dst = every.at[(left, right)[way], which]
        return pltpu.make_async_remote_copy(
            src_ref=src, dst_ref=dst, send_sem=block_s.at[way, step], recv_sem=block_r.at[way, step],
            device_id=(to, pair), device_id_type=MESH)

    for d in (1, 3, 2):
        tell(d).start()
    for step in range(2):
        for way in range(2):
            pass_on(way, step).start()
    mine_copy = pltpu.make_async_copy(blocks_ref, every.at[grp], own_s.at[0])
    mine_copy.start()
    for fetch in fetches[4:]:
        fetch.wait()
    pack_coef(occ_ref, vir_ref, coef_ref)

    def tables(d, carry):
        g = ring(grp - d, n_grp)

        @pl.when(d > 0)
        def _():
            tell(d).wait_recv()

        table_part(infos, g, per_dev, coef_ref, tab_h, tab_l, n_occ, n_vir)
        return carry

    lax.fori_loop(0, n_grp, tables, 0)
    for way in range(2):
        pass_on(way, 0).wait_recv()
        pass_on(way, 2).start()

    def turn(g, which):
        for j in range(which.start, which.stop):
            flip[g, j] = every[g, j].T

    mine_copy.wait()
    turn(grp, slice(0, per_dev))
    for way in range(2):
        pass_on(way, 1).wait_recv()
        turn((left, right)[way], slice(0, per_dev))
    for way in range(2):
        pass_on(way, 2).wait_recv()
        turn(far, parts_of[way])
    build_matrix(infos, every, flip, mat_h, mat_l, tiles_dev)
    share = chunk(grp, mine)

    def make_g(c, carry):
        cols = chunk(c, WIDE)
        g = dot3(tab_h[share, :], tab_l[share, :], mat_h[:, cols], mat_l[:, cols], NN)
        g = g.reshape(NZ * NY, NC, SUB, WIDE)
        for k in range(NC):
            kept = lax.rem(core + k + 1, NC)
            g_h[kept, :, cols], g_l[kept, :, cols] = split(g[:, k].reshape(NZ * NY * SUB, WIDE))
        return carry

    lax.fori_loop(0, rows // WIDE, make_g, 0)
    pieces = width // WIDE

    def over_core(p):
        return pltpu.make_async_remote_copy(
            src_ref=away.at[p], dst_ref=near.at[p], send_sem=core_s.at[p], recv_sem=core_r.at[p],
            device_id=at(z, y, 1 - core), device_id_type=MESH)

    def produce(p):
        tab = slice(p * WIDE, (p + 1) * WIDE)
        value = dot3(g_h[...].reshape(-1, rows), g_l[...].reshape(-1, rows), tab_h[tab, :], tab_l[tab, :], NT)
        value = value.reshape(NC, NZ, NY, SUB, WIDE)
        away[p] = value[0]
        own[p] = value[1]
        over_core(p).start()

    def settle(p):
        over_core(p).wait_recv()
        own[p] = own[p] + near[p]

    def chains(p, size, me, piece, landing, send, recv, to):
        hops = lengths(size)[p // 2 % 2]
        return [Chain(me, size, (1, -1)[d], hops[d], piece, landing.at[d], send.at[d], recv.at[d], to)
                for d in range(2)]

    first, second = [], []
    for p in range(pieces):
        i = p // 2
        if p % 2 == 0:
            first.append(chains(p, NZ, z, lambda v, p=p: own.at[p, v], z1.at[i], z1_s.at[i], z1_r.at[i], to_z))
            second.append([Direct(y, NY, lambda v, p=p: own.at[p, z, v], y2.at[i], y2_s.at[i], y2_r.at[i], to_y)])
        else:
            first.append(chains(p, NY, y, lambda v, p=p: own.at[p, :, v], y1.at[i], y1_s.at[i], y1_r.at[i], to_y))
            if i == 0:
                hops = lengths(NZ)[0]
                second.append([Chain(z, NZ, (1, -1)[d], hops[d], lambda v, p=p: own.at[p, v, y], zc.at[d], zc_s.at[d],
                                     zc_r.at[d], to_z) for d in range(2)])
            else:
                second.append([Direct(z, NZ, lambda v, p=p: own.at[p, v, y], z2, z2_s, z2_r, to_z)])

    def start(group):
        for way in group:
            way.start()

    def advance(p, j):
        for way in first[p]:
            way.advance(j)

    def turn_corner(p):
        here = own.at[p, z] if p % 2 == 0 else own.at[p, :, y]
        total = here[...]
        for way in first[p]:
            total = way.arrive(total)
        here[...] = total
        start(second[p])

    def go_on(j):
        for way in second[1]:
            way.advance(j)

    def finish(p):
        total = own[p, z, y]
        for way in second[p]:
            total = way.arrive(total)
        orb_out[:, p * WIDE : (p + 1) * WIDE] = total

    local = chunk(grp, rows // n_grp)

    def half_copy(c):
        cols = slice(c * WIDE, (c + 1) * WIDE)
        return pltpu.make_async_copy(half.at[:, cols], half_out.at[:, cols], half_s.at[c])

    def half_part(c):
        tab = slice(c * WIDE, (c + 1) * WIDE)
        half[:, tab] = dot3(mat_h[local, :], mat_l[local, :], tab_h[tab, :], tab_l[tab, :], NT)
        half_copy(c).start()

    produce(0)
    produce(1)
    settle(0)
    start(first[0])
    produce(2)
    settle(1)
    start(first[1])
    advance(0, 0)
    produce(3)
    settle(2)
    start(first[2])
    advance(1, 0)
    advance(0, 1)
    half_part(0)
    settle(3)
    start(first[3])
    half_part(1)
    advance(0, 2)
    advance(2, 0)
    half_part(2)
    turn_corner(1)
    advance(3, 0)
    advance(2, 1)
    half_part(3)
    turn_corner(0)
    go_on(0)
    advance(2, 2)
    turn_corner(3)
    go_on(1)
    turn_corner(2)
    go_on(2)
    for p in (0, 1, 3, 2):
        finish(p)

    for d in range(1, n_grp):
        tell(d).wait_send()
    for way in range(2):
        for step in range(3):
            pass_on(way, step).wait_send()
    for group in first + second:
        for way in group:
            way.drain()
    for p in range(pieces):
        over_core(p).wait_send()
        half_copy(p).wait()


def on_device(blocks, block_home, block_group, block_slot, pair_funcs, occ_coef, vir_coef):
    n_grp = lax.axis_size("grp")
    per_dev, tile, _ = blocks.shape
    rows_dev = pair_funcs.shape[1]
    tiles_dev = rows_dev // tile
    nb, n_occ = occ_coef.shape
    n_vir = vir_coef.shape[1]
    width = n_occ * n_vir
    rows = rows_dev * n_grp
    kept = NZ * NY * SUB
    pieces = width // WIDE
    vmem = pl.BlockSpec(memory_space=pltpu.VMEM)
    hbm = pl.BlockSpec(memory_space=pltpu.HBM)
    anywhere = pl.BlockSpec(memory_space=pl.ANY)
    dma = pltpu.SemaphoreType.DMA
    some = pieces // 2
    zh, yh = max(NZ // 2, 1), max(NY // 2, 1)
    return pl.pallas_call(
        functools.partial(column_kernel, n_vir, tiles_dev),
        out_shape=(jax.ShapeDtypeStruct((rows_dev, width), F32), jax.ShapeDtypeStruct((SUB, width), F32)),
        in_specs=[hbm] * 7,
        out_specs=(anywhere, vmem),
        scratch_shapes=[
            pltpu.SMEM((per_dev,), I32),
            pltpu.SMEM((per_dev,), I32),
            pltpu.SMEM((per_dev,), I32),
            pltpu.VMEM((2, rows_dev), I32),
            pltpu.VMEM((n_occ, nb), F32),
            pltpu.VMEM((nb, n_vir), F32),
            pltpu.VMEM((n_grp, INFO, rows_dev), I32),
            pltpu.VMEM((n_grp, per_dev, tile, tile), F32),
            pltpu.VMEM((n_grp, per_dev, tile, tile), F32),
            pltpu.VMEM((2 * (n_occ + n_vir), nb), BF16),
            pltpu.VMEM((width, rows), BF16),
            pltpu.VMEM((width, rows), BF16),
            pltpu.VMEM((rows, rows), BF16),
            pltpu.VMEM((rows, rows), BF16),
            pltpu.VMEM((NC, kept, rows), BF16),
            pltpu.VMEM((NC, kept, rows), BF16),
            pltpu.VMEM((pieces, NZ, NY, SUB, WIDE), F32),
            pltpu.VMEM((pieces, NZ, NY, SUB, WIDE), F32),
            pltpu.VMEM((pieces, NZ, NY, SUB, WIDE), F32),
            pltpu.VMEM((rows_dev, width), F32),
            pltpu.VMEM((some, 2, yh, NZ, SUB, WIDE), F32),
            pltpu.VMEM((some, 2, zh, NY, SUB, WIDE), F32),
            pltpu.VMEM((some, NY, SUB, WIDE), F32),
            pltpu.VMEM((NZ, SUB, WIDE), F32),
            pltpu.VMEM((2, zh, SUB, WIDE), F32),
            dma((n_grp,)), dma((n_grp,)), dma((2, 3)), dma((2, 3)), dma((7,)),
            dma((pieces,)), dma((pieces,)), dma((pieces,)),
            dma((some, 2, yh)), dma((some, 2, yh)), dma((some, 2, zh)), dma((some, 2, zh)),
            dma((some, NY)), dma((some, NY)), dma((NZ,)), dma((NZ,)), dma((2, zh)), dma((2, zh)),
        ],
        compiler_params=pltpu.CompilerParams(
            collective_id=0, has_side_effects=True, vmem_limit_bytes=VMEM_MIB * 2**20
        ),
    )(block_home, block_group.reshape(per_dev), block_slot, pair_funcs, occ_coef.T, vir_coef, blocks)


def solution(mesh):
    both = ("grp", "pair")
    placed = (P(both, None, None), P(both), P(both, None), P(both), P(None, both), P(), P())
    return jax.shard_map(
        on_device,
        mesh=mesh,
        in_specs=placed,
        out_specs=(P(both, None), P(both, None)),
        check_vma=False,
    )
```

```python
import functools

import jax
import jax.numpy as jnp
from jax import lax
from jax.experimental import pallas as pl
from jax.experimental.pallas import tpu as pltpu
from jax.sharding import PartitionSpec as P

F32, BF16, I32 = jnp.float32, jnp.bfloat16, jnp.int32
NZ, NY, NC = 8, 4, 2
STEP = 256
SUB = 8
INFO = 8
WIDE = 512
VMEM_MIB = 56
MESH = pl.DeviceIdType.MESH
NN, NT = ((1,), (0,)), ((1,), (1,))


def split(value):
    high = value.astype(BF16)
    return high, (value - high.astype(F32)).astype(BF16)


def dot(lhs, rhs, contract):
    return lax.dot_general(lhs, rhs, (contract, ((), ())), preferred_element_type=F32)


def dot3(lh, ll, rh, rl, contract):
    return dot(lh, rh, contract) + (dot(lh, rl, contract) + dot(ll, rh, contract))


def chunk(c, step=STEP):
    return pl.ds(pl.multiple_of(c * step, step), step)


def ring(i, n):
    return lax.rem(i + 2 * n, n)


class Chain:
    def __init__(self, me, size, sign, length, piece, landing, send_sem, recv_sem, to):
        self.me, self.size, self.sign, self.length = me, size, sign, length
        self.piece, self.landing, self.send_sem, self.recv_sem, self.to = piece, landing, send_sem, recv_sem, to

    def owner(self, j):
        return ring(self.me + self.sign * (self.length - j), self.size)

    def copy(self, j):
        return pltpu.make_async_remote_copy(
            src_ref=self.piece(self.owner(j)),
            dst_ref=self.landing.at[j],
            send_sem=self.send_sem.at[j],
            recv_sem=self.recv_sem.at[j],
            device_id=self.to(ring(self.me + self.sign, self.size)),
            device_id_type=MESH,
        )

    def start(self):
        if self.length:
            self.copy(0).start()

    def advance(self, j):
        if j < self.length - 1:
            self.copy(j).wait_recv()
            here = self.piece(self.owner(j + 1))
            here[...] = here[...] + self.landing[j]
            self.copy(j + 1).start()

    def arrive(self, total):
        if not self.length:
            return total
        self.copy(self.length - 1).wait_recv()
        return total + self.landing[self.length - 1]

    def drain(self):
        for j in range(self.length):
            self.copy(j).wait_send()


def lengths(n):
    far, near = n // 2, n - 1 - n // 2
    return ((far, near), (near, far))


def pack_coef(occ_ref, vir_ref, coef_ref):
    n_occ, n_vir = occ_ref.shape[0], vir_ref.shape[1]
    width = n_vir + n_occ
    coef_ref[:n_vir], coef_ref[width : width + n_vir] = split(vir_ref[...].T)
    coef_ref[n_vir:width], coef_ref[width + n_vir :] = split(occ_ref[...])


def table_part(info_ref, g, first, coef_ref, tab_h, tab_l, n_occ, n_vir):
    nb = coef_ref.shape[1]
    width = n_vir + n_occ
    got = []
    for f in range(2):
        func = info_ref[g, first + f : first + f + 1, :]
        hot = lax.broadcasted_iota(I32, (nb, STEP), 0) == func
        hot = jnp.where(hot, 1.0, 0.0).astype(BF16)
        both = dot(coef_ref[...], hot, NN)
        got.append(both[:width] + both[width:])
    (vir_p, occ_p), (vir_q, occ_q) = [(v[:n_vir], v[n_vir:]) for v in got]
    cols = chunk(g)
    for i in range(n_occ):
        entry = occ_p[i : i + 1] * vir_q + occ_q[i : i + 1] * vir_p
        high, low = split(entry)
        tab_h[i * n_vir : (i + 1) * n_vir, cols] = high
        tab_l[i * n_vir : (i + 1) * n_vir, cols] = low


def build_matrix(info_ref, every, mat_h, mat_l, tiles_dev):
    n_grp, per_dev, tile, _ = every.shape
    n_tiles = n_grp * tiles_dev

    def direct(h, t):
        dev = lax.div(h, tiles_dev)
        total = jnp.zeros((tile, tile), F32)
        for j in range(per_dev):
            code = info_ref[dev, j : j + 1, :]
            here = jnp.logical_and(code[:, :tile] == h, code[:, tile:] == t)
            total = total + jnp.where(here, every[dev, j], 0.0)
        return total

    def store(value, h, t):
        high, low = split(value)
        mat_h[chunk(h, tile), chunk(t, tile)] = high
        mat_l[chunk(h, tile), chunk(t, tile)] = low

    def body(step, carry):
        h = lax.rem(step, n_tiles)
        t = lax.rem(h + lax.div(step, n_tiles), n_tiles)
        value = direct(h, t) + direct(t, h).T
        store(value, h, t)
        store(value.T, t, h)
        return carry

    lax.fori_loop(0, n_tiles * (n_tiles + 1) // 2, body, 0)


class Direct:
    def __init__(self, me, size, piece, landing, send_sem, recv_sem, to):
        self.me, self.size, self.piece, self.landing = me, size, piece, landing
        self.send_sem, self.recv_sem, self.to = send_sem, recv_sem, to

    def copy(self, d):
        peer = ring(self.me + d, self.size)
        return pltpu.make_async_remote_copy(
            src_ref=self.piece(peer),
            dst_ref=self.landing.at[d],
            send_sem=self.send_sem.at[d],
            recv_sem=self.recv_sem.at[d],
            device_id=self.to(peer),
            device_id_type=MESH,
        )

    def order(self):
        return sorted(range(1, self.size), key=lambda d: -min(d, self.size - d))

    def start(self):
        for d in self.order():
            self.copy(d).start()

    def arrive(self, total):
        for d in reversed(self.order()):
            self.copy(d).wait_recv()
            total = total + self.landing[d]
        return total

    def drain(self):
        for d in range(1, self.size):
            self.copy(d).wait_send()


def column_kernel(n_vir, tiles_dev, home_in, group_in, slot_in, funcs_in, occ_in, vir_in, blocks_ref,
                  half_out, orb_out, home_ref, group_ref, slot_ref, funcs_ref, occ_ref, vir_ref, infos, every, coef_ref, tab_h, tab_l, mat_h, mat_l, g_h, g_l,
                  away, near, own, half, y1, z1, y2, z2, zc,
                  info_s, info_r, block_s, block_r, own_s, core_s, core_r, half_s,
                  y1_s, y1_r, z1_s, z1_r, y2_s, y2_r, z2_s, z2_r, zc_s, zc_r):
    n_grp, per_dev, tile, _ = every.shape
    n_occ = occ_ref.shape[0]
    width, rows = tab_h.shape
    mine = width // n_grp
    grp, pair = lax.axis_index("grp"), lax.axis_index("pair")
    core = lax.rem(pair, NC)
    y = lax.rem(lax.div(pair, NC), NY)
    z = lax.div(pair, NC * NY)
    right, left = ring(grp + 1, n_grp), ring(grp - 1, n_grp)

    def at(z_, y_, core_):
        return (grp, (z_ * NY + y_) * NC + core_)

    def to_y(v):
        return at(z, v, core)

    def to_z(v):
        return at(v, y, core)

    peers = [(ring(grp + d, n_grp), pair) for d in range(1, n_grp)]
    peers += [at(z, y, 1 - core)]
    peers += [to_y(ring(y + d, NY)) for d in range(1, NY)]
    peers += [to_z(ring(z + d, NZ)) for d in range(1, NZ)]
    pairs = ((home_in, home_ref), (group_in, group_ref), (slot_in, slot_ref), (funcs_in, funcs_ref),
             (occ_in, occ_ref), (vir_in, vir_ref))
    fetches = [pltpu.make_async_copy(src, dst, own_s.at[1 + i]) for i, (src, dst) in enumerate(pairs)]
    for fetch in fetches:
        fetch.start()
    barrier = pltpu.get_barrier_semaphore()
    for peer in peers:
        pl.semaphore_signal(barrier, inc=1, device_id=peer, device_id_type=MESH)
    for fetch in fetches[:4]:
        fetch.wait()
    lane = lax.broadcasted_iota(I32, (1, STEP), 1)
    for j in range(per_dev):
        home = grp * tiles_dev + home_ref[j]
        partner = group_ref[j] * tiles_dev + slot_ref[j]
        infos[grp, j : j + 1, :] = jnp.where(lane < tile, home, partner)
    infos[grp, per_dev : per_dev + 2, :] = funcs_ref[...]
    infos[grp, per_dev + 2 :, :] = jnp.zeros((INFO - per_dev - 2, STEP), I32)
    pl.semaphore_wait(barrier, len(peers))

    def tell(d):
        return pltpu.make_async_remote_copy(
            src_ref=infos.at[grp], dst_ref=infos.at[grp], send_sem=info_s.at[d], recv_sem=info_r.at[d],
            device_id=(ring(grp + d, n_grp), pair), device_id_type=MESH)

    split_at = per_dev // 2
    parts_of = (slice(0, split_at), slice(split_at, per_dev))

    def pass_on(way, step):
        to = (right, left)[way]
        which = parts_of[way if step != 1 else 1 - way]
        if step < 2:
            src, dst = blocks_ref.at[which], every.at[grp, which]
        else:
            src = dst = every.at[(left, right)[way], which]
        return pltpu.make_async_remote_copy(
            src_ref=src, dst_ref=dst, send_sem=block_s.at[way, step], recv_sem=block_r.at[way, step],
            device_id=(to, pair), device_id_type=MESH)

    for d in (1, 3, 2):
        tell(d).start()
    for step in range(2):
        for way in range(2):
            pass_on(way, step).start()
    mine_copy = pltpu.make_async_copy(blocks_ref, every.at[grp], own_s.at[0])
    mine_copy.start()
    for fetch in fetches[4:]:
        fetch.wait()
    pack_coef(occ_ref, vir_ref, coef_ref)

    def tables(d, carry):
        g = ring(grp - d, n_grp)

        @pl.when(d > 0)
        def _():
            tell(d).wait_recv()

        table_part(infos, g, per_dev, coef_ref, tab_h, tab_l, n_occ, n_vir)
        return carry

    lax.fori_loop(0, n_grp, tables, 0)
    for way in range(2):
        pass_on(way, 0).wait_recv()
        pass_on(way, 2).start()

    mine_copy.wait()
    for step in (1, 2):
        for way in range(2):
            pass_on(way, step).wait_recv()
    build_matrix(infos, every, mat_h, mat_l, tiles_dev)
    share = chunk(grp, mine)

    def make_g(c, carry):
        cols = chunk(c, WIDE)
        g = dot3(tab_h[share, :], tab_l[share, :], mat_h[:, cols], mat_l[:, cols], NN)
        g = g.reshape(NZ * NY, NC, SUB, WIDE)
        for k in range(NC):
            kept = lax.rem(core + k + 1, NC)
            g_h[kept, :, cols], g_l[kept, :, cols] = split(g[:, k].reshape(NZ * NY * SUB, WIDE))
        return carry

    lax.fori_loop(0, rows // WIDE, make_g, 0)
    pieces = width // WIDE

    def over_core(p):
        return pltpu.make_async_remote_copy(
            src_ref=away.at[p], dst_ref=near.at[p], send_sem=core_s.at[p], recv_sem=core_r.at[p],
            device_id=at(z, y, 1 - core), device_id_type=MESH)

    def produce(p):
        tab = slice(p * WIDE, (p + 1) * WIDE)
        value = dot3(g_h[...].reshape(-1, rows), g_l[...].reshape(-1, rows), tab_h[tab, :], tab_l[tab, :], NT)
        value = value.reshape(NC, NZ, NY, SUB, WIDE)
        away[p] = value[0]
        own[p] = value[1]
        over_core(p).start()

    def settle(p):
        over_core(p).wait_recv()
        own[p] = own[p] + near[p]

    def chains(p, size, me, piece, landing, send, recv, to):
        hops = lengths(size)[p // 2 % 2]
        return [Chain(me, size, (1, -1)[d], hops[d], piece, landing.at[d], send.at[d], recv.at[d], to)
                for d in range(2)]

    first, second = [], []
    for p in range(pieces):
        i = p // 2
        if p % 2 == 0:
            first.append(chains(p, NZ, z, lambda v, p=p: own.at[p, v], z1.at[i], z1_s.at[i], z1_r.at[i], to_z))
            second.append([Direct(y, NY, lambda v, p=p: own.at[p, z, v], y2.at[i], y2_s.at[i], y2_r.at[i], to_y)])
        else:
            first.append(chains(p, NY, y, lambda v, p=p: own.at[p, :, v], y1.at[i], y1_s.at[i], y1_r.at[i], to_y))
            if i == 0:
                hops = lengths(NZ)[0]
                second.append([Chain(z, NZ, (1, -1)[d], hops[d], lambda v, p=p: own.at[p, v, y], zc.at[d], zc_s.at[d],
                                     zc_r.at[d], to_z) for d in range(2)])
            else:
                second.append([Direct(z, NZ, lambda v, p=p: own.at[p, v, y], z2, z2_s, z2_r, to_z)])

    def start(group):
        for way in group:
            way.start()

    def advance(p, j):
        for way in first[p]:
            way.advance(j)

    def turn_corner(p):
        here = own.at[p, z] if p % 2 == 0 else own.at[p, :, y]
        total = here[...]
        for way in first[p]:
            total = way.arrive(total)
        here[...] = total
        start(second[p])

    def go_on(j):
        for way in second[1]:
            way.advance(j)

    def finish(p):
        total = own[p, z, y]
        for way in second[p]:
            total = way.arrive(total)
        orb_out[:, p * WIDE : (p + 1) * WIDE] = total

    local = chunk(grp, rows // n_grp)

    def half_copy(c):
        cols = slice(c * WIDE, (c + 1) * WIDE)
        return pltpu.make_async_copy(half.at[:, cols], half_out.at[:, cols], half_s.at[c])

    def half_part(c):
        tab = slice(c * WIDE, (c + 1) * WIDE)
        half[:, tab] = dot3(mat_h[local, :], mat_l[local, :], tab_h[tab, :], tab_l[tab, :], NT)
        half_copy(c).start()

    produce(0)
    produce(1)
    settle(0)
    start(first[0])
    produce(2)
    settle(1)
    start(first[1])
    advance(0, 0)
    produce(3)
    settle(2)
    start(first[2])
    advance(1, 0)
    advance(0, 1)
    half_part(0)
    settle(3)
    start(first[3])
    half_part(1)
    advance(0, 2)
    advance(2, 0)
    half_part(2)
    turn_corner(1)
    advance(3, 0)
    advance(2, 1)
    half_part(3)
    turn_corner(0)
    go_on(0)
    advance(2, 2)
    turn_corner(3)
    go_on(1)
    turn_corner(2)
    go_on(2)
    for p in (0, 1, 3, 2):
        finish(p)

    for d in range(1, n_grp):
        tell(d).wait_send()
    for way in range(2):
        for step in range(3):
            pass_on(way, step).wait_send()
    for group in first + second:
        for way in group:
            way.drain()
    for p in range(pieces):
        over_core(p).wait_send()
        half_copy(p).wait()


def on_device(blocks, block_home, block_group, block_slot, pair_funcs, occ_coef, vir_coef):
    n_grp = lax.axis_size("grp")
    per_dev, tile, _ = blocks.shape
    rows_dev = pair_funcs.shape[1]
    tiles_dev = rows_dev // tile
    nb, n_occ = occ_coef.shape
    n_vir = vir_coef.shape[1]
    width = n_occ * n_vir
    rows = rows_dev * n_grp
    kept = NZ * NY * SUB
    pieces = width // WIDE
    vmem = pl.BlockSpec(memory_space=pltpu.VMEM)
    hbm = pl.BlockSpec(memory_space=pltpu.HBM)
    anywhere = pl.BlockSpec(memory_space=pl.ANY)
    dma = pltpu.SemaphoreType.DMA
    some = pieces // 2
    zh, yh = max(NZ // 2, 1), max(NY // 2, 1)
    return pl.pallas_call(
        functools.partial(column_kernel, n_vir, tiles_dev),
        out_shape=(jax.ShapeDtypeStruct((rows_dev, width), F32), jax.ShapeDtypeStruct((SUB, width), F32)),
        in_specs=[hbm] * 7,
        out_specs=(anywhere, vmem),
        scratch_shapes=[
            pltpu.SMEM((per_dev,), I32),
            pltpu.SMEM((per_dev,), I32),
            pltpu.SMEM((per_dev,), I32),
            pltpu.VMEM((2, rows_dev), I32),
            pltpu.VMEM((n_occ, nb), F32),
            pltpu.VMEM((nb, n_vir), F32),
            pltpu.VMEM((n_grp, INFO, rows_dev), I32),
            pltpu.VMEM((n_grp, per_dev, tile, tile), F32),
            pltpu.VMEM((2 * (n_occ + n_vir), nb), BF16),
            pltpu.VMEM((width, rows), BF16),
            pltpu.VMEM((width, rows), BF16),
            pltpu.VMEM((rows, rows), BF16),
            pltpu.VMEM((rows, rows), BF16),
            pltpu.VMEM((NC, kept, rows), BF16),
            pltpu.VMEM((NC, kept, rows), BF16),
            pltpu.VMEM((pieces, NZ, NY, SUB, WIDE), F32),
            pltpu.VMEM((pieces, NZ, NY, SUB, WIDE), F32),
            pltpu.VMEM((pieces, NZ, NY, SUB, WIDE), F32),
            pltpu.VMEM((rows_dev, width), F32),
            pltpu.VMEM((some, 2, yh, NZ, SUB, WIDE), F32),
            pltpu.VMEM((some, 2, zh, NY, SUB, WIDE), F32),
            pltpu.VMEM((some, NY, SUB, WIDE), F32),
            pltpu.VMEM((NZ, SUB, WIDE), F32),
            pltpu.VMEM((2, zh, SUB, WIDE), F32),
            dma((n_grp,)), dma((n_grp,)), dma((2, 3)), dma((2, 3)), dma((7,)),
            dma((pieces,)), dma((pieces,)), dma((pieces,)),
            dma((some, 2, yh)), dma((some, 2, yh)), dma((some, 2, zh)), dma((some, 2, zh)),
            dma((some, NY)), dma((some, NY)), dma((NZ,)), dma((NZ,)), dma((2, zh)), dma((2, zh)),
        ],
        compiler_params=pltpu.CompilerParams(
            collective_id=0, has_side_effects=True, vmem_limit_bytes=VMEM_MIB * 2**20
        ),
    )(block_home, block_group.reshape(per_dev), block_slot, pair_funcs, occ_coef.T, vir_coef, blocks)


def solution(mesh):
    both = ("grp", "pair")
    placed = (P(both, None, None), P(both), P(both, None), P(both), P(None, both), P(), P())
    return jax.shard_map(
        on_device,
        mesh=mesh,
        in_specs=placed,
        out_specs=(P(both, None), P(both, None)),
        check_vma=False,
    )
```
